256 devices in a mesh: seq: 32 (over y_hi, z, core), tp: 8 (over y_lo, x).
Axes of the slice: x: 4, y: 4 (y_hi: 2, y_lo: 2; y = y_hi * 2 + y_lo), z: 8, core: 2. Of those that a mesh axis runs over, the one named last changes fastest.
Arguments:
- prompt: bfloat16 [4096, 5376], P(('seq', 'tp'))
- answers: bfloat16 [32, 64, 5376], P('seq', 'tp')
- answer_lengths: int32 [32], P('seq'), may hold values from 1 to 64, as said below
- input_gain: float32 [5376], replicated, may hold values from 0.1 to 1.9
- query_weight: bfloat16 [5376, 4096], P('seq', 'tp'), may hold values from -0.078125 to 0.078125
- key_weight: bfloat16 [5376, 2048], P('seq', 'tp'), may hold values from -0.078125 to 0.078125
- value_weight: bfloat16 [5376, 2048], P('seq', 'tp'), may hold values from -0.078125 to 0.078125
- query_gain: float32 [128], replicated, may hold values from 0.1 to 1.9
- key_gain: float32 [128], replicated, may hold values from 0.1 to 1.9
- out_weight: bfloat16 [4096, 5376], P(('tp', 'seq')), may hold values from -0.09375 to 0.09375
- post_gain: float32 [5376], replicated, may hold values from 0.1 to 1.9
Outputs:
- prompt_out: bfloat16 [4096, 5376], P(('seq', 'tp'))
- answer_out: bfloat16 [32, 64, 5376], P('seq', 'tp')
The draws below stay inside these ranges and needn't reach their ends.
Inputs may be any that keep to these rules, and one draw needn't show every extreme that they name: `answer_lengths`: some candidate has 64 live tokens and some has 1.
All inputs are finite; a program needn't handle non-finite values.
Results may differ from the reference program's by a relative error of at most 0.015.
Values may be sent and summed in bfloat16 or wider, within the bound.
A program may use at most 64 MiB of HBM per device.

```python
import jax
import jax.numpy as jnp
from jax import lax

D = 5376
HEADS = 32
KV_HEADS = 16
HEAD_DIM = 128
WINDOW = 1024
TOK_DEV = 128
ANS_LEN = 64
TOKENS = 4096
CANDS = 32
N_SEQ = 32
N_TP = 8


def activation_scales(key, shape, row_spread):
    first, second, third = jax.random.split(key, 3)
    row_scale = jnp.exp(jax.random.uniform(first, shape[:-1] + (1,), jnp.float32, -row_spread, row_spread))
    col_scale = jnp.exp(jax.random.uniform(second, (shape[-1],), jnp.float32, -1.15, 1.15)) / 1.5
    return (row_scale, col_scale, third)


def activation_values(key, shape):
    row_scale, col_scale, third = activation_scales(key, shape, 0.7)
    values = row_scale * col_scale * jax.random.normal(third, shape, jnp.float32)
    return values.astype(jnp.bfloat16)


def draw_prompt(key, part):
    key = jax.random.fold_in(key, 11)
    return activation_values(key, (TOKENS, D))


def draw_answers(key, part):
    key = jax.random.fold_in(key, 12)
    return activation_values(key, (CANDS, ANS_LEN, D))


def draw_answer_lengths(key, part):
    key = jax.random.fold_in(key, 13)
    first, second = jax.random.split(key)
    lengths = jax.random.randint(first, (CANDS,), 1, ANS_LEN + 1, dtype=jnp.int32)
    order = jax.random.permutation(second, CANDS)
    lengths = lengths.at[order[0]].set(ANS_LEN).at[order[1]].set(1)
    return lengths.astype(jnp.int32)


def block_scale(rng, extent, cuts, smallest, high):
    factor_of, own = 1.0, jax.random.fold_in(rng, 6)
    for dim, parts in cuts:
        heights = jnp.exp(jax.random.uniform(jax.random.fold_in(own, dim), (parts,), jnp.float32, smallest / len(cuts), high / len(cuts)))
        factor_of = factor_of * jnp.repeat(heights, extent[dim] // parts).reshape([-1 if axis == dim else 1 for axis in range(len(extent))])
    return factor_of


def bell_draw(rng, dims, spread, most, cuts=(), kind=jnp.bfloat16):
    values = jax.random.normal(rng, dims, jnp.float32) * spread
    if len(cuts) > 0:
        values = block_scale(rng, dims, cuts, -0.22, 0.18) * values
    return jnp.clip(values, min=-most, max=most).astype(kind)


def setup_inputs(seed: int = 0) -> dict:
    key_of = jax.random.split(jax.random.key(seed), 12)
    prompt = draw_prompt(jax.random.fold_in(key_of[11], 71), 0)
    answers = draw_answers(jax.random.fold_in(key_of[11], 71), 0)
    answer_lengths = draw_answer_lengths(jax.random.fold_in(key_of[11], 71), 0)
    input_gain = jnp.clip(1.0 + 0.18 * jax.random.normal(key_of[3], (D,), jnp.float32), 0.1, 1.9)
    query_weight = bell_draw(key_of[4], (D, HEADS * HEAD_DIM), D ** -0.5, 0.078125, ((0, 32), (1, 8)))
    key_weight = bell_draw(key_of[5], (D, KV_HEADS * HEAD_DIM), D ** -0.5, 0.078125, ((0, 32), (1, 8)))
    value_weight = bell_draw(key_of[6], (D, KV_HEADS * HEAD_DIM), D ** -0.5, 0.078125, ((0, 32), (1, 8)))
    query_gain = jnp.clip(1.0 + 0.18 * jax.random.normal(key_of[7], (HEAD_DIM,), jnp.float32), 0.1, 1.9)
    key_gain = jnp.clip(1.0 + 0.18 * jax.random.normal(key_of[8], (HEAD_DIM,), jnp.float32), 0.1, 1.9)
    out_weight = bell_draw(key_of[9], (HEADS * HEAD_DIM, D), (HEADS * HEAD_DIM) ** -0.5, 0.09375, ((0, 256),))
    post_gain = jnp.clip(1.0 + 0.18 * jax.random.normal(key_of[10], (D,), jnp.float32), 0.1, 1.9)
    return dict(prompt=prompt, answers=answers, answer_lengths=answer_lengths, input_gain=input_gain, query_weight=query_weight, key_weight=key_weight, value_weight=value_weight, query_gain=query_gain, key_gain=key_gain, out_weight=out_weight, post_gain=post_gain)


epsilon = 1e-06
query_scale = 168.0 ** (-0.5)

def rms_norm(inputs, gains):
    mean_square = lax.optimization_barrier(jnp.mean(inputs * inputs, axis=-1, keepdims=True))
    return inputs * lax.rsqrt(mean_square + epsilon) * gains

def stored(inputs):
    return lax.optimization_barrier(inputs.astype(jnp.bfloat16)).astype(jnp.float32)

def attend(query_rows, key_rows, value_rows, visible):
    row_count = query_rows.shape[0]
    group_size = HEADS // KV_HEADS
    grouped = query_rows.reshape(row_count, KV_HEADS, group_size, HEAD_DIM)
    scores = jnp.einsum('nkgd,mkd->kgnm', grouped, key_rows)
    weights = jnp.where(visible[None, None], jnp.exp(scores), 0.0)
    totals = lax.optimization_barrier(jnp.sum(weights, axis=-1))
    summed = jnp.einsum('kgnm,mkd->nkgd', stored(weights), value_rows)
    result = summed / jnp.transpose(totals, (2, 0, 1))[:, :, :, None]
    return result.reshape(row_count, HEADS * HEAD_DIM)

def reference(prompt, answers, answer_lengths, input_gain, query_weight, key_weight, value_weight, query_gain, key_gain, out_weight, post_gain):
    answer_rows = CANDS * ANS_LEN
    stacked = jnp.concatenate([prompt, answers.reshape(answer_rows, D)], 0)
    total_rows = stacked.shape[0]
    normed = rms_norm(stacked.astype(jnp.float32), input_gain.astype(jnp.float32)).astype(jnp.bfloat16)
    query_raw = jnp.dot(normed, query_weight, preferred_element_type=jnp.float32)
    key_raw = jnp.dot(normed, key_weight, preferred_element_type=jnp.float32)
    value_raw = jnp.dot(normed, value_weight, preferred_element_type=jnp.float32)
    queries = stored(rms_norm(query_raw.reshape(total_rows, HEADS, HEAD_DIM), query_gain.astype(jnp.float32)) * query_scale)
    keys = stored(rms_norm(key_raw.reshape(total_rows, KV_HEADS, HEAD_DIM), key_gain.astype(jnp.float32)))
    values = stored(value_raw).reshape(total_rows, KV_HEADS, HEAD_DIM)
    reach = WINDOW // TOK_DEV
    margin = reach * TOK_DEV
    prompt_keys = jnp.concatenate([jnp.zeros((margin, KV_HEADS, HEAD_DIM), jnp.float32), keys[:TOKENS]], 0)
    prompt_values = jnp.concatenate([jnp.zeros((margin, KV_HEADS, HEAD_DIM), jnp.float32), values[:TOKENS]], 0)
    prompt_queries = queries[:TOKENS].reshape(N_SEQ, TOK_DEV, HEADS, HEAD_DIM)

    def prompt_block(items):
        block_index, block_queries = items
        start = block_index * TOK_DEV
        block_keys = lax.dynamic_slice_in_dim(prompt_keys, start, margin + TOK_DEV, 0)
        block_values = lax.dynamic_slice_in_dim(prompt_values, start, margin + TOK_DEV, 0)
        query_pos = start + jnp.arange(TOK_DEV, dtype=jnp.int32)
        key_pos = start - margin + jnp.arange(margin + TOK_DEV, dtype=jnp.int32)
        visible = (key_pos[None, :] >= 0) & (key_pos[None, :] <= query_pos[:, None]) & (key_pos[None, :] > query_pos[:, None] - WINDOW)
        return stored(attend(block_queries, block_keys, block_values, visible))
    prompt_attention = lax.map(prompt_block, (jnp.arange(N_SEQ, dtype=jnp.int32), prompt_queries))
    prompt_attention = prompt_attention.reshape(TOKENS, HEADS * HEAD_DIM)
    window_keys = keys[TOKENS - WINDOW:TOKENS]
    window_values = values[TOKENS - WINDOW:TOKENS]
    answer_pos = jnp.arange(ANS_LEN, dtype=jnp.int32)[:, None]
    window_seen = jnp.arange(WINDOW, dtype=jnp.int32)[None, :] > answer_pos
    own_seen = jnp.arange(ANS_LEN, dtype=jnp.int32)[None, :] <= answer_pos
    answer_visible = jnp.concatenate([window_seen, own_seen], 1)

    def answer_block(items):
        cand_queries, cand_keys, cand_values = items
        all_keys = jnp.concatenate([window_keys, cand_keys], 0)
        all_values = jnp.concatenate([window_values, cand_values], 0)
        return stored(attend(cand_queries, all_keys, all_values, answer_visible))
    answer_attention = lax.map(answer_block, (queries[TOKENS:].reshape(CANDS, ANS_LEN, HEADS, HEAD_DIM), keys[TOKENS:].reshape(CANDS, ANS_LEN, KV_HEADS, HEAD_DIM), values[TOKENS:].reshape(CANDS, ANS_LEN, KV_HEADS, HEAD_DIM)))
    attention = jnp.concatenate([prompt_attention, answer_attention.reshape(answer_rows, HEADS * HEAD_DIM)], 0).astype(jnp.bfloat16)
    group_cols = HEADS * HEAD_DIM // N_TP
    mixed = jnp.zeros((total_rows, D), jnp.float32)
    for group_index in range(N_TP):
        lower = group_index * group_cols
        partial_term = jnp.dot(attention[:, lower:lower + group_cols], out_weight[lower:lower + group_cols], preferred_element_type=jnp.float32)
        mixed = mixed + stored(partial_term)
    branch = rms_norm(mixed, post_gain.astype(jnp.float32))
    prompt_out = (prompt.astype(jnp.float32) + branch[:TOKENS]).astype(jnp.bfloat16)
    answer_sum = answers.astype(jnp.float32) + branch[TOKENS:].reshape(CANDS, ANS_LEN, D)
    live = jnp.arange(ANS_LEN, dtype=jnp.int32)[None, :] < answer_lengths[:, None]
    answer_out = jnp.where(live[:, :, None], answer_sum, 0.0).astype(jnp.bfloat16)
    return (prompt_out, answer_out)
```

```python
import jax
import jax.numpy as jnp
from jax import lax
from jax.experimental import pallas as pl
from jax.experimental.pallas import tpu as pltpu
from jax.sharding import PartitionSpec as P

D = 5376
HALF = D // 2
HEAD = 128
ROWS_W = 168
PAIR_W = 2 * ROWS_W
PAD_W = 176
EPS = 1e-06
QUERY_SCALE = 168.0 ** (-0.5)
KC = 384

bf16 = jnp.bfloat16
f32 = jnp.float32

AG = ((0, 640, "x"), (640, 640, "y"), (1280, 640, "x"), (1920, 768, "y"))
RS = (
    (0, 512, "x"),
    (512, 512, "y"),
    (1024, 512, "x"),
    (1536, 512, "y"),
    (2048, 256, "x"),
    (2304, 384, "y"),
)
ORDER = (1, 3, 2)


def kernel(
    prompt,
    answers,
    lens,
    in_gain,
    wq,
    wk,
    wv,
    q_gain,
    k_gain,
    wo,
    post_gain,
    p_out,
    a_out,
    st,
    rx,
    wg,
    xg,
    acc,
    kvg,
    akv,
    qp,
    qa,
    num,
    tot,
    att,
    og,
    sb,
    r1,
    s2,
    r2,
    mix,
    e_ss,
    e_rs,
    w_ss,
    w_rs,
    o_ss,
    o_rs,
    kv_ss,
    kv_rs,
    ag_ss,
    ag_rs,
    r1_ss,
    r1_rs,
    r2_ss,
    r2_rs,
):
    seq = lax.axis_index("seq")
    tp = lax.axis_index("tp")
    yh, z, c = seq // 16, (seq // 2) % 8, seq % 2
    yl, x = tp // 4, tp % 4
    y = yh * 2 + yl

    def dev(y_, x_, z_, c_):
        return ((y_ // 2) * 16 + z_ * 2 + c_, (y_ % 2) * 4 + x_)

    sib = dev(y, x, z, 1 - c)
    z_fwd = dev(y, x, (z + 1) % 8, c)
    z_bwd = dev(y, x, (z + 7) % 8, c)
    diag = dev((y + 2) % 4, x, z, 1 - c)

    def peer(axis, d):
        if axis == "x":
            return dev(y, (x + d) % 4, z, c)
        return dev((y + d) % 4, x, z, c)

    partners = [sib, z_fwd, z_bwd, diag] + [peer(a, d) for a in "xy" for d in ORDER]
    barrier = pltpu.get_barrier_semaphore()
    for target in partners:
        pl.semaphore_signal(
            barrier, inc=1, device_id=target, device_id_type=pl.DeviceIdType.MESH
        )

    started = []

    def send(src, dst, send_sem, recv_sem, target):
        copy = pltpu.make_async_remote_copy(
            src_ref=src,
            dst_ref=dst,
            send_sem=send_sem,
            recv_sem=recv_sem,
            device_id=target,
            device_id_type=pl.DeviceIdType.MESH,
        )
        copy.start()
        started.append(copy)

    def arrived(dst, send_sem, recv_sem):
        pltpu.make_async_remote_copy(
            src_ref=dst,
            dst_ref=dst,
            send_sem=send_sem,
            recv_sem=recv_sem,
            device_id=sib,
            device_id_type=pl.DeviceIdType.MESH,
        ).wait_recv()

    for h in range(2):
        st[h, 0, :ROWS_W, :] = wq[:, 256 * h : 256 * h + 256]
        st[h, 1, :ROWS_W, :128] = wk[:, 128 * h : 128 * h + 128]
        st[h, 1, :ROWS_W, 128:] = wv[:, 128 * h : 128 * h + 128]
    pl.semaphore_wait(barrier, len(partners))
    send(st.at[yh, 1 - c], rx.at[0], e_ss.at[0], e_rs.at[0], sib)
    send(st.at[1 - yh, c], rx.at[1], e_ss.at[1], e_rs.at[1], peer("y", 2))
    send(st.at[1 - yh, 1 - c], rx.at[2], e_ss.at[2], e_rs.at[2], diag)

    gain = in_gain[...]
    rows = prompt[...].astype(f32)
    rows = rows * lax.rsqrt(jnp.mean(rows * rows, axis=-1, keepdims=True) + EPS) * gain
    xg[y, x, 0:16, :] = rows[:, :HALF].astype(bf16)
    xg[y, x, 16:32, :] = rows[:, HALF:].astype(bf16)
    rows = answers[...].astype(f32)
    rows = rows * lax.rsqrt(jnp.mean(rows * rows, axis=-1, keepdims=True) + EPS) * gain
    xg[y, x, 32:48, :] = jnp.concatenate([rows[:, :HALF], rows[:, HALF:]], 0).astype(bf16)

    def ag_one(q, y_, x_):
        start, width, _ = AG[q]
        return xg.at[y_, x_, :, pl.ds(start, width)]

    def ag_line(q, k):
        start, width, axis = AG[q]
        if axis == "x":
            return xg.at[k, :, :, pl.ds(start, width)]
        return xg.at[:, k, :, pl.ds(start, width)]

    def ag_first(q):
        axis = AG[q][2]
        for d in ORDER:
            send(
                ag_one(q, y, x),
                ag_one(q, y, x),
                ag_ss.at[q, 0, d - 1],
                ag_rs.at[q, 0, d - 1],
                peer(axis, d),
            )

    def ag_second(q):
        axis = AG[q][2]
        for d in ORDER:
            if axis == "x":
                piece = ag_one(q, y, (x + 4 - d) % 4)
            else:
                piece = ag_one(q, (y + 4 - d) % 4, x)
            arrived(piece, ag_ss.at[q, 0, d - 1], ag_rs.at[q, 0, d - 1])
        mine = ag_line(q, y if axis == "x" else x)
        for d in ORDER:
            send(
                mine,
                mine,
                ag_ss.at[q, 1, d - 1],
                ag_rs.at[q, 1, d - 1],
                peer("y" if axis == "x" else "x", d),
            )

    def ag_done(q):
        axis = AG[q][2]
        own = y if axis == "x" else x
        for d in ORDER:
            arrived(
                ag_line(q, (own + 4 - d) % 4), ag_ss.at[q, 1, d - 1], ag_rs.at[q, 1, d - 1]
            )

    for q in range(len(AG)):
        ag_first(q)

    def w_block(core, m):
        return wg.at[core, pl.ds(pl.multiple_of(m * PAIR_W, 16), PAIR_W), :]

    def w_index(h, dz):
        return ((yh + h) % 2) * 8 + (z + dz) % 8

    def w_send(m, way, target):
        send(w_block(c, m), w_block(c, m), w_ss.at[way, m], w_rs.at[c, m], target)

    def pair_up(h, mine, other):
        low = jnp.where(c == 0, mine, other)
        high = jnp.where(c == 0, other, mine)
        m = w_index(h, 0)
        wg[c, pl.ds(pl.multiple_of(m * PAIR_W, 16), PAIR_W), :] = jnp.concatenate(
            [low, high], 0
        ).astype(bf16)
        w_send(m, 0, z_fwd)
        w_send(m, 1, z_bwd)
        w_send(m, 2, sib)

    arrived(rx.at[0], e_ss.at[0], e_rs.at[0])
    pair_up(
        0,
        st[yh, c, :ROWS_W, :].astype(f32),
        rx[0, :ROWS_W, :].astype(f32),
    )
    arrived(rx.at[1], e_ss.at[1], e_rs.at[1])
    arrived(rx.at[2], e_ss.at[2], e_rs.at[2])
    pair_up(1, rx[1, :ROWS_W, :].astype(f32), rx[2, :ROWS_W, :].astype(f32))

    def w_pass(h, k, way):
        m = w_index(h, 8 - k if way == 0 else k)
        arrived(w_block(c, m), w_ss.at[2, m], w_rs.at[c, m])
        if k < (4 if h == way else 3):
            w_send(m, way, z_fwd if way == 0 else z_bwd)
        w_send(m, 2, sib)

    def w_step(k):
        for h in range(2):
            for way in range(2):
                if k <= (4 if h == way else 3):
                    w_pass(h, k, way)

    def o_send(slot, way, target):
        send(og.at[slot], og.at[slot], o_ss.at[way, slot], o_rs.at[slot], target)

    def o_start():
        slot = z * 2 + c
        og[slot] = wo[...]
        o_send(slot, 0, z_fwd)
        o_send(slot, 1, z_bwd)
        o_send(slot, 2, sib)

    def o_step(k):
        for way in range(2):
            reach = 3 if way == 0 else 4
            if k <= reach:
                slot = ((z + (8 - k if way == 0 else k)) % 8) * 2 + c
                arrived(og.at[slot], o_ss.at[2, slot], o_rs.at[slot])
                if k < reach:
                    o_send(slot, way, z_fwd if way == 0 else z_bwd)
                o_send(slot, 2, sib)

    for q in range(len(AG)):
        ag_second(q)
    for k in range(1, 5):
        w_step(k)
        if k == 3:
            o_start()
    for q in range(len(AG)):
        ag_done(q)
    for m in range(16):
        arrived(w_block(1 - c, m), w_ss.at[2, m], w_rs.at[1 - c, m])

    def project(core):
        acc[...] = jnp.zeros_like(acc)
        for h in range(2):

            def body(i, carry):
                cols = pl.ds(pl.multiple_of(i * KC, 128), KC)
                ask = xg[:, :, 16 * h : 16 * h + 16, cols].reshape(256, KC)
                tail = xg[:, :, 32:48, cols].astype(f32)
                tail = tail[:, :, 8 * h : 8 * h + 8, :].reshape(128, KC).astype(bf16)
                krows = pl.ds(pl.multiple_of(h * HALF + i * KC, 128), KC)
                acc[...] += jnp.dot(
                    jnp.concatenate([ask, tail], 0),
                    wg[core, krows, :],
                    preferred_element_type=f32,
                )
                return carry

            lax.fori_loop(0, HALF // KC, body, 0)

    def head_norm(raw, gains):
        return raw * lax.rsqrt(jnp.mean(raw * raw, axis=-1, keepdims=True) + EPS) * gains

    o_step(1)
    project(1)
    keys = head_norm(acc[:, :128], k_gain[...]).astype(bf16)
    values = acc[:, 128:].astype(bf16)
    for g in range(2):
        kvg[g, z, c, :, :128] = keys[g * 128 : (g + 1) * 128]
        kvg[g, z, c, :, 128:] = values[g * 128 : (g + 1) * 128]
    akv[:, :128] = keys[256:]
    akv[:, 128:] = values[256:]

    def kv_send(g, zs, way, target):
        piece = kvg.at[g, zs, c]
        send(piece, piece, kv_ss.at[way, g, zs], kv_rs.at[g, zs, c], target)

    for g in range(2):
        kv_send(g, z, 0, z_fwd)
        kv_send(g, z, 2, sib)
    kv_send(1, z, 1, z_bwd)

    o_step(2)
    project(0)
    for h in range(2):
        raw = acc[:, 128 * h : 128 * h + 128]
        normed = (head_norm(raw, q_gain[...]) * QUERY_SCALE).astype(bf16)
        for g in range(2):
            qp[g, h * 128 : (h + 1) * 128, :] = normed[g * 128 : (g + 1) * 128]
        for e in range(2):
            low = e * 128 + h * 64
            qa[low : low + 64, :] = normed[256 + e * 64 : 320 + e * 64]

    def scored(queries, keys_):
        return jnp.exp(
            lax.dot_general(
                queries, keys_, (((1,), (1,)), ((), ())), preferred_element_type=f32
            )
        )

    def add_in(slot, weights, values_):
        part = weights[:, :128]
        if weights.shape[1] == 256:
            part = part + weights[:, 128:]
        tot[slot] += part
        num[slot] += jnp.dot(weights.astype(bf16), values_, preferred_element_type=f32)

    num[...] = jnp.zeros_like(num)
    tot[...] = jnp.zeros_like(tot)

    row_ = lax.broadcasted_iota(jnp.int32, (256, 128), 0)
    col_ = lax.broadcasted_iota(jnp.int32, (256, 128), 1)
    own = scored(qa[...], akv[:, :128])
    own_seen = (row_ // 128 == col_ // 64) & (col_ % 64 <= row_ % 64)
    add_in(2, jnp.where(own_seen, own, 0.0), akv[:, 128:])

    row = lax.broadcasted_iota(jnp.int32, (256, 256), 0)
    col = lax.broadcasted_iota(jnp.int32, (256, 256), 1)

    def prompt_step(k):
        zs = (z + 8 - k) % 8
        ahead = c * 128 + 256 * k + row % 128 - col

        def one(g, source):
            pair = kvg[source, zs].reshape(256, 256)
            weights = scored(qp[g], pair[:, :128])
            if k == 0:
                weights = jnp.where(ahead >= 0, weights, 0.0)
            if k == 4:
                weights = jnp.where(ahead < 1024, weights, 0.0)
            add_in(g, weights, pair[:, 128:])

        if k == 0:
            one(0, 0)
            one(1, 1)
        else:

            @pl.when(z >= k)
            def _():
                one(0, 0)

            one(1, (z + 8 - k) // 8)

    def kv_sib(g, zs):
        arrived(kvg.at[g, zs, 1 - c], kv_ss.at[2, g, zs], kv_rs.at[g, zs, 1 - c])

    kv_sib(0, z)
    kv_sib(1, z)
    prompt_step(0)
    for k in range(1, 5):
        zs = (z + 8 - k) % 8
        zn = (z + k) % 8
        for g in range(2):
            arrived(kvg.at[g, zs, c], kv_ss.at[2, g, zs], kv_rs.at[g, zs, c])
            if k < 4:
                kv_send(g, zs, 0, z_fwd)
            kv_send(g, zs, 2, sib)
        if k < 4:
            arrived(kvg.at[1, zn, c], kv_ss.at[2, 1, zn], kv_rs.at[1, zn, c])
            if k < 3:
                kv_send(1, zn, 1, z_bwd)
            kv_send(1, zn, 2, sib)
        if k < 3:
            o_step(k + 2)
        for g in range(2):
            kv_sib(g, zs)
        if k < 4:
            kv_sib(1, zn)
        prompt_step(k)

    for zz in range(4, 8):
        pair = kvg[1, zz].reshape(256, 256)
        weights = scored(qa[...], pair[:, :128])
        if zz == 4:
            weights = jnp.where(col > row % 64, weights, 0.0)
        add_in(2, weights, pair[:, 128:])

    for g in range(2):
        out = num[g] / jnp.sum(tot[g], axis=-1, keepdims=True)
        for h in range(2):
            att[g * 128 : (g + 1) * 128, h * 128 : (h + 1) * 128] = out[
                h * 128 : (h + 1) * 128
            ].astype(bf16)
    out = num[2] / jnp.sum(tot[2], axis=-1, keepdims=True)
    for e in range(2):
        for h in range(2):
            low = e * 128 + h * 64
            att[256 + e * 64 : 320 + e * 64, h * 128 : (h + 1) * 128] = out[
                low : low + 64
            ].astype(bf16)

    for zz in range(8):
        slot = zz * 2 + 1 - c
        arrived(og.at[slot], o_ss.at[2, slot], o_rs.at[slot])

    for q, (start, width, axis) in enumerate(RS):
        cols = slice(start, start + width)
        left = jnp.dot(
            att[...],
            og[:, :, start : start + width].reshape(256, width),
            preferred_element_type=f32,
        )
        right = jnp.dot(
            att[...],
            og[:, :, HALF + start : HALF + start + width].reshape(256, width),
            preferred_element_type=f32,
        )
        for y_ in range(4):
            for x_ in range(4):
                i, j = (x_, y_) if axis == "x" else (y_, x_)
                p = y_ * 4 + x_
                sb[i, j, 0:16, cols] = left[p * 16 : p * 16 + 16].astype(bf16)
                sb[i, j, 16:32, cols] = right[p * 16 : p * 16 + 16].astype(bf16)
                low = 256 + p * 8
                sb[i, j, 32:48, cols] = jnp.concatenate(
                    [left[low : low + 8], right[low : low + 8]], 0
                ).astype(bf16)
        mi = x if axis == "x" else y
        for d in ORDER:
            send(
                sb.at[(mi + d) % 4, :, :, pl.ds(start, width)],
                r1.at[d - 1, :, :, pl.ds(start, width)],
                r1_ss.at[q, d - 1],
                r1_rs.at[q, d - 1],
                peer(axis, d),
            )
    for q, (start, width, axis) in enumerate(RS):
        cols = slice(start, start + width)
        mi, mj = (x, y) if axis == "x" else (y, x)
        for d in ORDER:
            arrived(
                r1.at[d - 1, :, :, pl.ds(start, width)],
                r1_ss.at[q, d - 1],
                r1_rs.at[q, d - 1],
            )
        total = sb[mi, :, :, cols].astype(f32)
        for d in range(3):
            total = total + r1[d, :, :, cols].astype(f32)
        s2[:, :, cols] = total.astype(bf16)
        for d in ORDER:
            send(
                s2.at[(mj + d) % 4, :, pl.ds(start, width)],
                r2.at[d - 1, :, pl.ds(start, width)],
                r2_ss.at[q, d - 1],
                r2_rs.at[q, d - 1],
                peer("y" if axis == "x" else "x", d),
            )
    for q, (start, width, axis) in enumerate(RS):
        cols = slice(start, start + width)
        mj = y if axis == "x" else x
        for d in ORDER:
            arrived(
                r2.at[d - 1, :, pl.ds(start, width)],
                r2_ss.at[q, d - 1],
                r2_rs.at[q, d - 1],
            )
        total = s2[mj, :, cols].astype(f32)
        for d in range(3):
            total = total + r2[d, :, cols].astype(f32)
        mix[:, cols] = total

    def square_sum(part):
        return jnp.sum(part * part, axis=-1, keepdims=True)

    left, right = mix[0:16, :], mix[16:32, :]
    scale = lax.rsqrt((square_sum(left) + square_sum(right)) / D + EPS)
    p_out[:, :HALF] = (
        prompt[:, :HALF].astype(f32) + left * scale * post_gain[:, :HALF]
    ).astype(bf16)
    p_out[:, HALF:] = (
        prompt[:, HALF:].astype(f32) + right * scale * post_gain[:, HALF:]
    ).astype(bf16)
    left, right = mix[32:40, :], mix[40:48, :]
    scale = lax.rsqrt((square_sum(left) + square_sum(right)) / D + EPS)
    position = tp * 8 + lax.broadcasted_iota(jnp.int32, (8, HALF), 0)
    live = position < lens[0]
    a_out[:, :HALF] = jnp.where(
        live, answers[:, :HALF].astype(f32) + left * scale * post_gain[:, :HALF], 0.0
    ).astype(bf16)
    a_out[:, HALF:] = jnp.where(
        live, answers[:, HALF:].astype(f32) + right * scale * post_gain[:, HALF:], 0.0
    ).astype(bf16)

    for copy in started:
        copy.wait_send()


def on_device(
    prompt,
    answers,
    answer_lengths,
    input_gain,
    query_weight,
    key_weight,
    value_weight,
    query_gain,
    key_gain,
    out_weight,
    post_gain,
):
    vmem = pl.BlockSpec(memory_space=pltpu.VMEM)
    dma = pltpu.SemaphoreType.DMA
    n_ag, n_rs = len(AG), len(RS)
    prompt_out, answer_out = pl.pallas_call(
        kernel,
        out_shape=(
            jax.ShapeDtypeStruct((16, D), bf16),
            jax.ShapeDtypeStruct((8, D), bf16),
        ),
        in_specs=[vmem, vmem, pl.BlockSpec(memory_space=pltpu.SMEM)] + [vmem] * 8,
        out_specs=(vmem, vmem),
        scratch_shapes=[
            pltpu.VMEM((2, 2, PAD_W, 256), bf16),
            pltpu.VMEM((3, PAD_W, 256), bf16),
            pltpu.VMEM((2, D, 256), bf16),
            pltpu.VMEM((4, 4, 48, HALF), bf16),
            pltpu.VMEM((384, 256), f32),
            pltpu.VMEM((2, 8, 2, 128, 256), bf16),
            pltpu.VMEM((128, 256), bf16),
            pltpu.VMEM((2, 256, 128), bf16),
            pltpu.VMEM((256, 128), bf16),
            pltpu.VMEM((3, 256, 128), f32),
            pltpu.VMEM((3, 256, 128), f32),
            pltpu.VMEM((384, 256), bf16),
            pltpu.VMEM((16, 16, D), bf16),
            pltpu.VMEM((4, 4, 48, HALF), bf16),
            pltpu.VMEM((3, 4, 48, HALF), bf16),
            pltpu.VMEM((4, 48, HALF), bf16),
            pltpu.VMEM((3, 48, HALF), bf16),
            pltpu.VMEM((48, HALF), f32),
            dma((3,)),
            dma((3,)),
            dma((3, 16)),
            dma((2, 16)),
            dma((3, 16)),
            dma((16,)),
            dma((3, 2, 8)),
            dma((2, 8, 2)),
            dma((n_ag, 2, 3)),
            dma((n_ag, 2, 3)),
            dma((n_rs, 3)),
            dma((n_rs, 3)),
            dma((n_rs, 3)),
            dma((n_rs, 3)),
        ],
        compiler_params=pltpu.CompilerParams(
            collective_id=0, has_side_effects=True, vmem_limit_bytes=56 * 1024 * 1024
        ),
        name="sublayer",
    )(
        prompt,
        answers[0],
        answer_lengths,
        input_gain[None],
        query_weight,
        key_weight,
        value_weight,
        query_gain[None],
        key_gain[None],
        out_weight,
        post_gain[None],
    )
    return prompt_out, answer_out[None]


def solution(mesh):
    placed = (
        P(("seq", "tp"), None),
        P("seq", "tp", None),
        P("seq"),
        P(),
        P("seq", "tp"),
        P("seq", "tp"),
        P("seq", "tp"),
        P(),
        P(),
        P(("tp", "seq"), None),
        P(),
    )
    return jax.shard_map(
        on_device,
        mesh=mesh,
        in_specs=placed,
        out_specs=(P(("seq", "tp"), None), P("seq", "tp", None)),
        check_vma=False,
    )
```

```python
import jax
import jax.numpy as jnp
from jax import lax
from jax.experimental import pallas as pl
from jax.experimental.pallas import tpu as pltpu
from jax.sharding import PartitionSpec as P

D = 5376
HALF = D // 2
HEAD = 128
ROWS_W = 168
PAIR_W = 2 * ROWS_W
PAD_W = 176
EPS = 1e-06
QUERY_SCALE = 168.0 ** (-0.5)
KC = 896

bf16 = jnp.bfloat16
f32 = jnp.float32

AG = (
    (0, 32, 0, 640, "x"),
    (0, 32, 640, 640, "y"),
    (0, 32, 1280, 640, "x"),
    (0, 32, 1920, 768, "y"),
    (32, 16, 0, 1280, "x"),
    (32, 16, 1280, 1408, "y"),
)
RS = (
    (0, 384, "x"),
    (384, 512, "y"),
    (896, 512, "x"),
    (1408, 384, "y"),
    (1792, 384, "x"),
    (2176, 512, "y"),
)
ORDER = (1, 3, 2)
O_REACH = (2, 5)


def kernel(
    prompt,
    answers,
    lens,
    in_gain,
    wq,
    wk,
    wv,
    q_gain,
    k_gain,
    wo,
    post_gain,
    p_out,
    a_out,
    st,
    rx,
    wg,
    xg,
    acc,
    kvg,
    akv,
    qp,
    qa,
    num,
    tot,
    att,
    og,
    sb,
    ra,
    r1,
    s2,
    r2,
    mix,
    e_ss,
    e_rs,
    w_ss,
    w_rs,
    o_ss,
    o_rs,
    kv_ss,
    kv_rs,
    ag_ss,
    ag_rs,
    rs_ss,
    rs_rs,
):
    seq = lax.axis_index("seq")
    tp = lax.axis_index("tp")
    yh, z, c = seq // 16, (seq // 2) % 8, seq % 2
    yl, x = tp // 4, tp % 4
    y = yh * 2 + yl

    def dev(y_, x_, z_, c_):
        return ((y_ // 2) * 16 + z_ * 2 + c_, (y_ % 2) * 4 + x_)

    sib = dev(y, x, z, 1 - c)
    z_to = (dev(y, x, (z + 1) % 8, c), dev(y, x, (z + 7) % 8, c))
    diag = dev((y + 2) % 4, x, z, 1 - c)

    def peer(axis, d):
        if axis == "x":
            return dev(y, (x + d) % 4, z, c)
        return dev((y + d) % 4, x, z, c)

    partners = [sib, *z_to, diag] + [peer(a, d) for a in "xy" for d in ORDER]
    barrier = pltpu.get_barrier_semaphore()
    for target in partners:
        pl.semaphore_signal(
            barrier, inc=1, device_id=target, device_id_type=pl.DeviceIdType.MESH
        )

    started = []

    def send(src, dst, send_sem, recv_sem, target):
        copy = pltpu.make_async_remote_copy(
            src_ref=src,
            dst_ref=dst,
            send_sem=send_sem,
            recv_sem=recv_sem,
            device_id=target,
            device_id_type=pl.DeviceIdType.MESH,
        )
        copy.start()
        started.append(copy)

    def arrived(dst, recv_sem):
        pltpu.make_async_remote_copy(
            src_ref=dst,
            dst_ref=dst,
            send_sem=e_ss.at[0, 0],
            recv_sem=recv_sem,
            device_id=sib,
            device_id_type=pl.DeviceIdType.MESH,
        ).wait_recv()

    for h in range(2):
        st[h, 0, 0, :ROWS_W, :] = wk[:, 128 * h : 128 * h + 128]
        st[h, 0, 1, :ROWS_W, :] = wv[:, 128 * h : 128 * h + 128]
        for i in range(2):
            low = 256 * h + 128 * i
            st[h, 1, i, :ROWS_W, :] = wq[:, low : low + 128]
    pl.semaphore_wait(barrier, len(partners))
    for f in range(2):
        send(st.at[yh, f, 1 - c], rx.at[f, 0], e_ss.at[f, 0], e_rs.at[f, 0], sib)
        send(
            st.at[1 - yh, f, c], rx.at[f, 1], e_ss.at[f, 1], e_rs.at[f, 1], peer("y", 2)
        )
        send(st.at[1 - yh, f, 1 - c], rx.at[f, 2], e_ss.at[f, 2], e_rs.at[f, 2], diag)

    def ag_one(q, y_, x_):
        row, count, start, width, _ = AG[q]
        return xg.at[y_, x_, pl.ds(row, count), pl.ds(start, width)]

    def ag_line(q, k):
        row, count, start, width, axis = AG[q]
        rows_, cols_ = pl.ds(row, count), pl.ds(start, width)
        if axis == "x":
            return xg.at[k, :, rows_, cols_]
        return xg.at[:, k, rows_, cols_]

    def ag_axes(q):
        if AG[q][4] == "x":
            return "x", "y", x, y
        return "y", "x", y, x

    def ag_a(q):
        first, _, _, _ = ag_axes(q)
        mine = ag_one(q, y, x)
        for d in ORDER:
            send(mine, mine, ag_ss.at[q, d - 1], ag_rs.at[q, d - 1], peer(first, d))

    def ag_b(q):
        first, second, _, own = ag_axes(q)
        for d in ORDER:
            if first == "x":
                piece = ag_one(q, y, (x + 4 - d) % 4)
            else:
                piece = ag_one(q, (y + 4 - d) % 4, x)
            arrived(piece, ag_rs.at[q, d - 1])
        mine = ag_line(q, own)
        for d in ORDER:
            send(mine, mine, ag_ss.at[q, 2 + d], ag_rs.at[q, 2 + d], peer(second, d))

    def ag_done(q):
        _, _, _, own = ag_axes(q)
        for d in ORDER:
            arrived(ag_line(q, (own + 4 - d) % 4), ag_rs.at[q, 2 + d])

    def w_block(f, core, m):
        return wg.at[2 * f + core, pl.ds(pl.multiple_of(m * PAIR_W, 16), PAIR_W), :]

    def w_index(h, dz):
        return ((yh + h) % 2) * 8 + (z + dz) % 8

    def w_send(f, m, way):
        piece = w_block(f, c, m)
        target = sib if way == 2 else z_to[way]
        send(piece, piece, w_ss.at[f, way, m], w_rs.at[f, c, m], target)

    def w_own(f, h):
        if h == 0:
            arrived(rx.at[f, 0], e_rs.at[f, 0])
            mine = st[yh, f, c, :ROWS_W, :].astype(f32)
            other = rx[f, 0, :ROWS_W, :].astype(f32)
        else:
            arrived(rx.at[f, 1], e_rs.at[f, 1])
            arrived(rx.at[f, 2], e_rs.at[f, 2])
            mine = rx[f, 1, :ROWS_W, :].astype(f32)
            other = rx[f, 2, :ROWS_W, :].astype(f32)
        low = jnp.where(c == 0, mine, other)
        high = jnp.where(c == 0, other, mine)
        m = w_index(h, 0)
        wg[2 * f + c, pl.ds(pl.multiple_of(m * PAIR_W, 16), PAIR_W), :] = (
            jnp.concatenate([low, high], 0).astype(bf16)
        )
        for way in range(3):
            w_send(f, m, way)

    def w_step(f, k):
        for h in range(2):
            for way in range(2):
                reach = 4 if h == way else 3
                if k <= reach:
                    m = w_index(h, 8 - k if way == 0 else k)
                    arrived(w_block(f, c, m), w_rs.at[f, c, m])
                    if k < reach:
                        w_send(f, m, way)
                    w_send(f, m, 2)

    def w_done(f):
        for m in range(16):
            arrived(w_block(f, 1 - c, m), w_rs.at[f, 1 - c, m])

    def o_send(slot, way):
        piece = og.at[slot]
        target = sib if way == 2 else z_to[way]
        send(piece, piece, o_ss.at[way, slot], o_rs.at[slot], target)

    def o_start(*ways):
        for way in ways:
            o_send(z * 2 + c, way)

    def o_step(way, k):
        slot = ((z + (8 - k if way == 0 else k)) % 8) * 2 + c
        arrived(og.at[slot], o_rs.at[slot])
        if k < O_REACH[way]:
            o_send(slot, way)
        o_send(slot, 2)

    def o_done():
        for zz in range(8):
            slot = zz * 2 + 1 - c
            arrived(og.at[slot], o_rs.at[slot])

    def drain():
        while started:
            started.pop(0).wait_send()

    def kv_send(g, zs, way):
        piece = kvg.at[g, zs, c]
        target = sib if way == 2 else z_to[way]
        send(piece, piece, kv_ss.at[way, g, zs], kv_rs.at[g, zs, c], target)

    def kv_start():
        for g in range(2):
            kv_send(g, z, 0)
        kv_send(1, z, 1)
        for g in range(2):
            kv_send(g, z, 2)

    def kv_step(k):
        zs = (z + 8 - k) % 8
        zn = (z + k) % 8
        for g in range(2):
            arrived(kvg.at[g, zs, c], kv_rs.at[g, zs, c])
            if k < 4:
                kv_send(g, zs, 0)
            kv_send(g, zs, 2)
        if k < 4:
            arrived(kvg.at[1, zn, c], kv_rs.at[1, zn, c])
            if k < 3:
                kv_send(1, zn, 1)
            kv_send(1, zn, 2)

    def kv_done(k):
        zs = (z + 8 - k) % 8
        zn = (z + k) % 8
        for g in range(2):
            arrived(kvg.at[g, zs, 1 - c], kv_rs.at[g, zs, 1 - c])
        if 0 < k < 4:
            arrived(kvg.at[1, zn, 1 - c], kv_rs.at[1, zn, 1 - c])

    def project(f):
        acc[0:256, 256 * f : 256 * f + 256] = jnp.zeros((256, 256), f32)
        for h in range(2):

            def body(i, carry):
                cols_ = pl.ds(pl.multiple_of(i * KC, 128), KC)
                krows = pl.ds(pl.multiple_of(h * HALF + i * KC, 128), KC)
                acc[0:256, 256 * f : 256 * f + 256] += jnp.dot(
                    xg[:, :, 16 * h : 16 * h + 16, cols_].reshape(256, KC),
                    jnp.concatenate([wg[2 * f, krows, :], wg[2 * f + 1, krows, :]], 1),
                    preferred_element_type=f32,
                )
                return carry

            lax.fori_loop(0, HALF // KC, body, 0)

    def project_answers():
        acc[256:384, :] = jnp.zeros((128, 512), f32)
        for h in range(2):

            def body(i, carry):
                cols_ = pl.ds(pl.multiple_of(i * KC, 128), KC)
                krows = pl.ds(pl.multiple_of(h * HALF + i * KC, 128), KC)
                tail = xg[:, :, 32:48, cols_].astype(f32)
                tail = tail[:, :, 8 * h : 8 * h + 8, :].reshape(128, KC).astype(bf16)
                acc[256:384, :] += jnp.dot(
                    tail,
                    jnp.concatenate([wg[i_, krows, :] for i_ in range(4)], 1),
                    preferred_element_type=f32,
                )
                return carry

            lax.fori_loop(0, HALF // KC, body, 0)

    def head_norm(raw, gains):
        return raw * lax.rsqrt(jnp.mean(raw * raw, axis=-1, keepdims=True) + EPS) * gains

    def scored(queries, keys_):
        return jnp.exp(
            lax.dot_general(
                queries, keys_, (((1,), (1,)), ((), ())), preferred_element_type=f32
            )
        )

    def add_in(slot, weights, values_):
        part = weights[:, :128]
        if weights.shape[1] == 256:
            part = part + weights[:, 128:]
        tot[slot] += part
        num[slot] += jnp.dot(weights.astype(bf16), values_, preferred_element_type=f32)

    row = lax.broadcasted_iota(jnp.int32, (256, 256), 0)
    col = lax.broadcasted_iota(jnp.int32, (256, 256), 1)

    def prompt_step(k):
        zs = (z + 8 - k) % 8
        ahead = c * 128 + 256 * k + row % 128 - col

        def one(g, source):
            pair = kvg[source, zs].reshape(256, 256)
            weights = scored(qp[g], pair[:, :128])
            if k == 0:
                weights = jnp.where(ahead >= 0, weights, 0.0)
            if k == 4:
                weights = jnp.where(ahead < 1024, weights, 0.0)
            add_in(g, weights, pair[:, 128:])

        if k == 0:
            one(0, 0)
            one(1, 1)
        else:

            @pl.when(z >= k)
            def _():
                one(0, 0)

            one(1, (z + 8 - k) // 8)

    og[z * 2 + c] = wo[...]
    o_start(0, 1, 2)
    gain = in_gain[...].reshape(1, D)
    rows = prompt[...].astype(f32)
    rows = rows * lax.rsqrt(jnp.mean(rows * rows, axis=-1, keepdims=True) + EPS) * gain
    xg[y, x, 0:16, :] = rows[:, :HALF].astype(bf16)
    xg[y, x, 16:32, :] = rows[:, HALF:].astype(bf16)
    for q in range(4):
        ag_a(q)
    w_own(0, 0)
    rows = answers[...].astype(f32)
    rows = rows * lax.rsqrt(jnp.mean(rows * rows, axis=-1, keepdims=True) + EPS) * gain
    xg[y, x, 32:48, :] = jnp.concatenate([rows[:, :HALF], rows[:, HALF:]], 0).astype(bf16)
    ag_a(4)
    ag_a(5)
    w_own(0, 1)
    for q in range(4):
        ag_b(q)
    w_step(0, 1)
    w_own(1, 0)
    w_own(1, 1)
    w_step(0, 2)
    w_step(1, 1)
    w_step(0, 3)
    o_step(0, 1)
    o_step(1, 1)
    ag_b(4)
    ag_b(5)
    w_step(1, 2)
    w_step(0, 4)
    for q in range(4):
        ag_done(q)
    w_done(0)
    project(0)
    keys = head_norm(acc[0:256, :128], k_gain[...]).astype(bf16)
    values = acc[0:256, 128:256].astype(bf16)
    for g in range(2):
        kvg[g, z, c, :, :128] = keys[g * 128 : (g + 1) * 128]
        kvg[g, z, c, :, 128:] = values[g * 128 : (g + 1) * 128]
    kv_start()
    w_step(1, 3)
    o_step(1, 2)
    kv_step(1)
    w_step(1, 4)
    o_step(1, 3)
    o_step(0, 2)
    w_done(1)
    project(1)
    for h in range(2):
        raw = acc[0:256, 256 + 128 * h : 384 + 128 * h]
        normed = (head_norm(raw, q_gain[...]) * QUERY_SCALE).astype(bf16)
        for g in range(2):
            qp[g, h * 128 : (h + 1) * 128, :] = normed[g * 128 : (g + 1) * 128]
    kv_step(2)
    o_step(1, 4)
    num[...] = jnp.zeros_like(num)
    tot[...] = jnp.zeros_like(tot)
    kv_done(0)
    prompt_step(0)
    kv_done(1)
    prompt_step(1)
    for q in (4, 5):
        ag_done(q)
    project_answers()
    kv_step(3)
    keys = head_norm(acc[256:384, :128], k_gain[...]).astype(bf16)
    akv[:, :128] = keys
    akv[:, 128:] = acc[256:384, 128:256].astype(bf16)
    for h in range(2):
        raw = acc[256:384, 256 + 128 * h : 384 + 128 * h]
        normed = (head_norm(raw, q_gain[...]) * QUERY_SCALE).astype(bf16)
        for e in range(2):
            low = e * 128 + h * 64
            qa[low : low + 64, :] = normed[e * 64 : e * 64 + 64]
    kv_done(2)
    prompt_step(2)
    kv_step(4)
    row_ = lax.broadcasted_iota(jnp.int32, (256, 128), 0)
    col_ = lax.broadcasted_iota(jnp.int32, (256, 128), 1)
    own = scored(qa[...], akv[:, :128])
    own_seen = (row_ // 128 == col_ // 64) & (col_ % 64 <= row_ % 64)
    add_in(2, jnp.where(own_seen, own, 0.0), akv[:, 128:])
    kv_done(3)
    prompt_step(3)
    kv_done(4)
    prompt_step(4)
    for zz in range(4, 8):
        pair = kvg[1, zz].reshape(256, 256)
        weights = scored(qa[...], pair[:, :128])
        if zz == 4:
            weights = jnp.where(col > row % 64, weights, 0.0)
        add_in(2, weights, pair[:, 128:])


    o_step(1, 5)

    for g in range(2):
        out = num[g] / jnp.sum(tot[g], axis=-1, keepdims=True)
        for h in range(2):
            att[g * 128 : (g + 1) * 128, h * 128 : (h + 1) * 128] = out[
                h * 128 : (h + 1) * 128
            ].astype(bf16)
    out = num[2] / jnp.sum(tot[2], axis=-1, keepdims=True)
    for e in range(2):
        for h in range(2):
            low = e * 128 + h * 64
            att[256 + e * 64 : 320 + e * 64, h * 128 : (h + 1) * 128] = out[
                low : low + 64
            ].astype(bf16)

    def rs_axes(q):
        if RS[q][2] == "x":
            return "x", "y", x, y
        return "y", "x", y, x

    def rs_a(q):
        start, width, axis = RS[q]
        cols_ = slice(start, start + width)
        left = jnp.dot(
            att[...],
            og[:, :, start : start + width].reshape(256, width),
            preferred_element_type=f32,
        )
        right = jnp.dot(
            att[...],
            og[:, :, HALF + start : HALF + start + width].reshape(256, width),
            preferred_element_type=f32,
        )
        for y_ in range(4):
            for x_ in range(4):
                i, k = (x_, y_) if axis == "x" else (y_, x_)
                p = y_ * 4 + x_
                sb[i, k, 0:16, cols_] = left[p * 16 : p * 16 + 16].astype(bf16)
                sb[i, k, 16:32, cols_] = right[p * 16 : p * 16 + 16].astype(bf16)
                low_ = 256 + p * 8
                sb[i, k, 32:48, cols_] = jnp.concatenate(
                    [left[low_ : low_ + 8], right[low_ : low_ + 8]], 0
                ).astype(bf16)
        first, _, mi, _ = rs_axes(q)
        cols_ = pl.ds(start, width)
        for w, d in enumerate((1, 3)):
            send(
                sb.at[(mi + 2) % 4, pl.ds(2 * w, 2), :, cols_],
                ra.at[w, :, :, cols_],
                rs_ss.at[q, w],
                rs_rs.at[q, w],
                peer(first, d),
            )

    def rs_b(q):
        start, width, _ = RS[q]
        first, _, mi, _ = rs_axes(q)
        cols_ = slice(start, start + width)
        for w, d in enumerate((1, 3)):
            arrived(ra.at[w, :, :, pl.ds(start, width)], rs_rs.at[q, w])
            i = (mi + d) % 4
            sb[i, 2 * w : 2 * w + 2, :, cols_] = (
                sb[i, 2 * w : 2 * w + 2, :, cols_].astype(f32)
                + ra[w, :, :, cols_].astype(f32)
            ).astype(bf16)
            send(
                sb.at[i, :, :, pl.ds(start, width)],
                r1.at[w, :, :, pl.ds(start, width)],
                rs_ss.at[q, 2 + w],
                rs_rs.at[q, 2 + w],
                peer(first, d),
            )

    def rs_c(q):
        start, width, _ = RS[q]
        _, second, mi, mj = rs_axes(q)
        cols_ = slice(start, start + width)
        for w in range(2):
            arrived(r1.at[w, :, :, pl.ds(start, width)], rs_rs.at[q, 2 + w])
        s2[:, :, cols_] = (
            sb[mi, :, :, cols_].astype(f32)
            + r1[0, :, :, cols_].astype(f32)
            + r1[1, :, :, cols_].astype(f32)
        ).astype(bf16)
        for d in ORDER:
            send(
                s2.at[(mj + d) % 4, :, pl.ds(start, width)],
                r2.at[d - 1, :, pl.ds(start, width)],
                rs_ss.at[q, 3 + d],
                rs_rs.at[q, 3 + d],
                peer(second, d),
            )

    def rs_d(q):
        start, width, _ = RS[q]
        _, _, _, mj = rs_axes(q)
        cols_ = slice(start, start + width)
        for d in ORDER:
            arrived(r2.at[d - 1, :, pl.ds(start, width)], rs_rs.at[q, 3 + d])
        total = s2[mj, :, cols_].astype(f32)
        for d in range(3):
            total = total + r2[d, :, cols_].astype(f32)
        mix[:, cols_] = total

    o_done()
    for q in range(len(RS)):
        rs_a(q)
    drain()
    for q in range(len(RS)):
        rs_b(q)
    for q in range(len(RS)):
        rs_c(q)
    for q in range(len(RS)):
        rs_d(q)

    gain = post_gain[...].reshape(1, D)

    def square_sum(part):
        return jnp.sum(part * part, axis=-1, keepdims=True)

    left, right = mix[0:16, :], mix[16:32, :]
    scale = lax.rsqrt((square_sum(left) + square_sum(right)) / D + EPS)
    p_out[:, :HALF] = (
        prompt[:, :HALF].astype(f32) + left * scale * gain[:, :HALF]
    ).astype(bf16)
    p_out[:, HALF:] = (
        prompt[:, HALF:].astype(f32) + right * scale * gain[:, HALF:]
    ).astype(bf16)
    left, right = mix[32:40, :], mix[40:48, :]
    scale = lax.rsqrt((square_sum(left) + square_sum(right)) / D + EPS)
    position = tp * 8 + lax.broadcasted_iota(jnp.int32, (8, HALF), 0)
    live = position < lens[0]
    a_out[:, :HALF] = jnp.where(
        live, answers[:, :HALF].astype(f32) + left * scale * gain[:, :HALF], 0.0
    ).astype(bf16)
    a_out[:, HALF:] = jnp.where(
        live, answers[:, HALF:].astype(f32) + right * scale * gain[:, HALF:], 0.0
    ).astype(bf16)

    drain()


def on_device(
    prompt,
    answers,
    answer_lengths,
    input_gain,
    query_weight,
    key_weight,
    value_weight,
    query_gain,
    key_gain,
    out_weight,
    post_gain,
):
    vmem = pl.BlockSpec(memory_space=pltpu.VMEM)
    dma = pltpu.SemaphoreType.DMA
    n_ag, n_rs = len(AG), len(RS)
    prompt_out, answer_out = pl.pallas_call(
        kernel,
        out_shape=(
            jax.ShapeDtypeStruct((16, D), bf16),
            jax.ShapeDtypeStruct((8, D), bf16),
        ),
        in_specs=[vmem, vmem, pl.BlockSpec(memory_space=pltpu.SMEM)] + [vmem] * 8,
        out_specs=(vmem, vmem),
        scratch_shapes=[
            pltpu.VMEM((2, 2, 2, PAD_W, 128), bf16),
            pltpu.VMEM((2, 3, PAD_W, 128), bf16),
            pltpu.VMEM((4, D, 128), bf16),
            pltpu.VMEM((4, 4, 48, HALF), bf16),
            pltpu.VMEM((384, 512), f32),
            pltpu.VMEM((2, 8, 2, 128, 256), bf16),
            pltpu.VMEM((128, 256), bf16),
            pltpu.VMEM((2, 256, 128), bf16),
            pltpu.VMEM((256, 128), bf16),
            pltpu.VMEM((3, 256, 128), f32),
            pltpu.VMEM((3, 256, 128), f32),
            pltpu.VMEM((384, 256), bf16),
            pltpu.VMEM((16, 16, D), bf16),
            pltpu.VMEM((4, 4, 48, HALF), bf16),
            pltpu.VMEM((2, 2, 48, HALF), bf16),
            pltpu.VMEM((2, 4, 48, HALF), bf16),
            pltpu.VMEM((4, 48, HALF), bf16),
            pltpu.VMEM((3, 48, HALF), bf16),
            pltpu.VMEM((48, HALF), f32),
            dma((2, 3)),
            dma((2, 3)),
            dma((2, 3, 16)),
            dma((2, 2, 16)),
            dma((3, 16)),
            dma((16,)),
            dma((3, 2, 8)),
            dma((2, 8, 2)),
            dma((n_ag, 7)),
            dma((n_ag, 7)),
            dma((n_rs, 7)),
            dma((n_rs, 7)),
        ],
        compiler_params=pltpu.CompilerParams(
            collective_id=0, has_side_effects=True, vmem_limit_bytes=56 * 1024 * 1024
        ),
        name="sublayer",
    )(
        prompt,
        answers[0],
        answer_lengths,
        input_gain,
        query_weight,
        key_weight,
        value_weight,
        query_gain[None],
        key_gain[None],
        out_weight,
        post_gain,
    )
    return prompt_out, answer_out[None]


def solution(mesh):
    placed = (
        P(("seq", "tp"), None),
        P("seq", "tp", None),
        P("seq"),
        P(),
        P("seq", "tp"),
        P("seq", "tp"),
        P("seq", "tp"),
        P(),
        P(),
        P(("tp", "seq"), None),
        P(),
    )
    return jax.shard_map(
        on_device,
        mesh=mesh,
        in_specs=placed,
        out_specs=(P(("seq", "tp"), None), P("seq", "tp", None)),
        check_vma=False,
    )
```

```python
import jax
import jax.numpy as jnp
from jax import lax
from jax.experimental import pallas as pl
from jax.experimental.pallas import tpu as pltpu
from jax.sharding import PartitionSpec as P

D = 5376
HALF = D // 2
HEAD = 128
ROWS_W = 168
PAIR_W = 2 * ROWS_W
PAD_W = 176
EPS = 1e-06
QUERY_SCALE = 168.0 ** (-0.5)
KC = 896

bf16 = jnp.bfloat16
f32 = jnp.float32

AG = (
    (0, 32, 0, 1280, "x"),
    (0, 32, 1280, 1408, "y"),
    (32, 16, 0, 1280, "x"),
    (32, 16, 1280, 1408, "y"),
)
RS = ((0, 640, "x"), (640, 640, "y"), (1280, 640, "x"), (1920, 768, "y"))
ORDER = (1, 3, 2)
O_REACH = (3, 4)


def kernel(
    prompt,
    answers,
    lens,
    in_gain,
    wq,
    wk,
    wv,
    q_gain,
    k_gain,
    wo,
    post_gain,
    p_out,
    a_out,
    st,
    rx,
    wg,
    xg,
    acc,
    kvg,
    akv,
    qp,
    qa,
    num,
    tot,
    att,
    og,
    sb,
    ra,
    r1,
    s2,
    r2,
    mix,
    e_ss,
    e_rs,
    w_ss,
    w_rs,
    o_ss,
    o_rs,
    kv_ss,
    kv_rs,
    ag_ss,
    ag_rs,
    rs_ss,
    rs_rs,
):
    seq = lax.axis_index("seq")
    tp = lax.axis_index("tp")
    yh, z, c = seq // 16, (seq // 2) % 8, seq % 2
    yl, x = tp // 4, tp % 4
    y = yh * 2 + yl

    def dev(y_, x_, z_, c_):
        return ((y_ // 2) * 16 + z_ * 2 + c_, (y_ % 2) * 4 + x_)

    sib = dev(y, x, z, 1 - c)
    z_to = (dev(y, x, (z + 1) % 8, c), dev(y, x, (z + 7) % 8, c))
    diag = dev((y + 2) % 4, x, z, 1 - c)

    def peer(axis, d):
        if axis == "x":
            return dev(y, (x + d) % 4, z, c)
        return dev((y + d) % 4, x, z, c)

    partners = [sib, *z_to, diag] + [peer(a, d) for a in "xy" for d in ORDER]
    barrier = pltpu.get_barrier_semaphore()
    for target in partners:
        pl.semaphore_signal(
            barrier, inc=1, device_id=target, device_id_type=pl.DeviceIdType.MESH
        )

    started = []

    def send(src, dst, send_sem, recv_sem, target):
        copy = pltpu.make_async_remote_copy(
            src_ref=src,
            dst_ref=dst,
            send_sem=send_sem,
            recv_sem=recv_sem,
            device_id=target,
            device_id_type=pl.DeviceIdType.MESH,
        )
        copy.start()
        started.append(copy)

    def arrived(dst, recv_sem):
        pltpu.make_async_remote_copy(
            src_ref=dst,
            dst_ref=dst,
            send_sem=e_ss.at[0, 0],
            recv_sem=recv_sem,
            device_id=sib,
            device_id_type=pl.DeviceIdType.MESH,
        ).wait_recv()

    for h in range(2):
        st[h, 0, 0, :ROWS_W, :] = wk[:, 128 * h : 128 * h + 128]
        st[h, 0, 1, :ROWS_W, :] = wv[:, 128 * h : 128 * h + 128]
        for i in range(2):
            low = 256 * h + 128 * i
            st[h, 1, i, :ROWS_W, :] = wq[:, low : low + 128]
    gain = in_gain[...].reshape(1, D)
    rows = prompt[...].astype(f32)
    rows = rows * lax.rsqrt(jnp.mean(rows * rows, axis=-1, keepdims=True) + EPS) * gain
    xg[y, x, 0:16, :] = rows[:, :HALF].astype(bf16)
    xg[y, x, 16:32, :] = rows[:, HALF:].astype(bf16)
    rows = answers[...].astype(f32)
    rows = rows * lax.rsqrt(jnp.mean(rows * rows, axis=-1, keepdims=True) + EPS) * gain
    xg[y, x, 32:48, :] = jnp.concatenate([rows[:, :HALF], rows[:, HALF:]], 0).astype(bf16)
    pl.semaphore_wait(barrier, len(partners))
    def exchange(f):
        send(st.at[yh, f, 1 - c], rx.at[f, 0], e_ss.at[f, 0], e_rs.at[f, 0], sib)
        send(
            st.at[1 - yh, f, c], rx.at[f, 1], e_ss.at[f, 1], e_rs.at[f, 1], peer("y", 2)
        )
        send(st.at[1 - yh, f, 1 - c], rx.at[f, 2], e_ss.at[f, 2], e_rs.at[f, 2], diag)

    def ag_one(q, y_, x_):
        row, count, start, width, _ = AG[q]
        return xg.at[y_, x_, pl.ds(row, count), pl.ds(start, width)]

    def ag_line(q, k):
        row, count, start, width, axis = AG[q]
        rows_, cols_ = pl.ds(row, count), pl.ds(start, width)
        if axis == "x":
            return xg.at[k, :, rows_, cols_]
        return xg.at[:, k, rows_, cols_]

    def ag_axes(q):
        if AG[q][4] == "x":
            return "x", "y", x, y
        return "y", "x", y, x

    def ag_a(q):
        first, _, _, _ = ag_axes(q)
        mine = ag_one(q, y, x)
        for d in ORDER:
            send(mine, mine, ag_ss.at[q, d - 1], ag_rs.at[q, d - 1], peer(first, d))

    def ag_b(q):
        first, second, _, own = ag_axes(q)
        for d in ORDER:
            if first == "x":
                piece = ag_one(q, y, (x + 4 - d) % 4)
            else:
                piece = ag_one(q, (y + 4 - d) % 4, x)
            arrived(piece, ag_rs.at[q, d - 1])
        mine = ag_line(q, own)
        for d in ORDER:
            send(mine, mine, ag_ss.at[q, 2 + d], ag_rs.at[q, 2 + d], peer(second, d))

    def ag_done(q):
        _, _, _, own = ag_axes(q)
        for d in ORDER:
            arrived(ag_line(q, (own + 4 - d) % 4), ag_rs.at[q, 2 + d])

    def w_block(f, core, m):
        return wg.at[2 * f + core, pl.ds(pl.multiple_of(m * PAIR_W, 16), PAIR_W), :]

    def w_index(h, dz):
        return ((yh + h) % 2) * 8 + (z + dz) % 8

    def w_send(f, m, way):
        piece = w_block(f, c, m)
        target = sib if way == 2 else z_to[way]
        send(piece, piece, w_ss.at[f, way, m], w_rs.at[f, c, m], target)

    def w_own(f, h):
        if h == 0:
            arrived(rx.at[f, 0], e_rs.at[f, 0])
            mine = st[yh, f, c, :ROWS_W, :].astype(f32)
            other = rx[f, 0, :ROWS_W, :].astype(f32)
        else:
            arrived(rx.at[f, 1], e_rs.at[f, 1])
            arrived(rx.at[f, 2], e_rs.at[f, 2])
            mine = rx[f, 1, :ROWS_W, :].astype(f32)
            other = rx[f, 2, :ROWS_W, :].astype(f32)
        low = jnp.where(c == 0, mine, other)
        high = jnp.where(c == 0, other, mine)
        m = w_index(h, 0)
        wg[2 * f + c, pl.ds(pl.multiple_of(m * PAIR_W, 16), PAIR_W), :] = (
            jnp.concatenate([low, high], 0).astype(bf16)
        )
        for way in range(3):
            w_send(f, m, way)

    def w_step(f, k):
        for h in range(2):
            for way in range(2):
                reach = 4 if h == way else 3
                if k <= reach:
                    m = w_index(h, 8 - k if way == 0 else k)
                    arrived(w_block(f, c, m), w_rs.at[f, c, m])
                    if k < reach:
                        w_send(f, m, way)
                    w_send(f, m, 2)

    def w_done(f):
        for m in range(16):
            arrived(w_block(f, 1 - c, m), w_rs.at[f, 1 - c, m])

    def o_send(slot, way):
        piece = og.at[slot]
        target = sib if way == 2 else z_to[way]
        send(piece, piece, o_ss.at[way, slot], o_rs.at[slot], target)

    def o_start(*ways):
        for way in ways:
            o_send(z * 2 + c, way)

    def o_step(way, k):
        slot = ((z + (8 - k if way == 0 else k)) % 8) * 2 + c
        arrived(og.at[slot], o_rs.at[slot])
        if k < O_REACH[way]:
            o_send(slot, way)
        o_send(slot, 2)

    def o_done():
        for zz in range(8):
            slot = zz * 2 + 1 - c
            arrived(og.at[slot], o_rs.at[slot])

    def drain():
        while started:
            started.pop(0).wait_send()

    def kv_send(g, zs, way):
        piece = kvg.at[g, zs, c]
        target = sib if way == 2 else z_to[way]
        send(piece, piece, kv_ss.at[way, g, zs], kv_rs.at[g, zs, c], target)

    def kv_start():
        for g in range(2):
            kv_send(g, z, 0)
        kv_send(1, z, 1)
        for g in range(2):
            kv_send(g, z, 2)

    def kv_step(k):
        zs = (z + 8 - k) % 8
        zn = (z + k) % 8
        for g in range(2):
            if k < 4 or g == 0:
                arrived(kvg.at[g, zs, c], kv_rs.at[g, zs, c])
                if k < 4 - g:
                    kv_send(g, zs, 0)
                kv_send(g, zs, 2)
        arrived(kvg.at[1, zn, c], kv_rs.at[1, zn, c])
        if k < 4:
            kv_send(1, zn, 1)
        kv_send(1, zn, 2)

    def kv_done(k):
        zs = (z + 8 - k) % 8
        zn = (z + k) % 8
        for g in range(2):
            arrived(kvg.at[g, zs, 1 - c], kv_rs.at[g, zs, 1 - c])
        if 0 < k < 4:
            arrived(kvg.at[1, zn, 1 - c], kv_rs.at[1, zn, 1 - c])

    def project(f):
        acc[0:256, 256 * f : 256 * f + 256] = jnp.zeros((256, 256), f32)
        for h in range(2):

            def body(i, carry):
                cols_ = pl.ds(pl.multiple_of(i * KC, 128), KC)
                krows = pl.ds(pl.multiple_of(h * HALF + i * KC, 128), KC)
                acc[0:256, 256 * f : 256 * f + 256] += jnp.dot(
                    xg[:, :, 16 * h : 16 * h + 16, cols_].reshape(256, KC),
                    jnp.concatenate([wg[2 * f, krows, :], wg[2 * f + 1, krows, :]], 1),
                    preferred_element_type=f32,
                )
                return carry

            lax.fori_loop(0, HALF // KC, body, 0)

    def project_answers():
        acc[256:384, :] = jnp.zeros((128, 512), f32)
        for h in range(2):

            def body(i, carry):
                cols_ = pl.ds(pl.multiple_of(i * KC, 128), KC)
                krows = pl.ds(pl.multiple_of(h * HALF + i * KC, 128), KC)
                tail = xg[:, :, 32:48, cols_].astype(f32)
                tail = tail[:, :, 8 * h : 8 * h + 8, :].reshape(128, KC).astype(bf16)
                acc[256:384, :] += jnp.dot(
                    tail,
                    jnp.concatenate([wg[i_, krows, :] for i_ in range(4)], 1),
                    preferred_element_type=f32,
                )
                return carry

            lax.fori_loop(0, HALF // KC, body, 0)

    def head_norm(raw, gains):
        return raw * lax.rsqrt(jnp.mean(raw * raw, axis=-1, keepdims=True) + EPS) * gains

    def scored(queries, keys_):
        return jnp.exp(
            lax.dot_general(
                queries, keys_, (((1,), (1,)), ((), ())), preferred_element_type=f32
            )
        )

    def add_in(slot, weights, values_):
        part = weights[:, :128]
        if weights.shape[1] == 256:
            part = part + weights[:, 128:]
        tot[slot] += part
        num[slot] += jnp.dot(weights.astype(bf16), values_, preferred_element_type=f32)

    row = lax.broadcasted_iota(jnp.int32, (256, 256), 0)
    col = lax.broadcasted_iota(jnp.int32, (256, 256), 1)

    def prompt_step(k):
        zs = (z + 8 - k) % 8
        ahead = c * 128 + 256 * k + row % 128 - col

        def one(g, source):
            pair = kvg[source, zs].reshape(256, 256)
            weights = scored(qp[g], pair[:, :128])
            if k == 0:
                weights = jnp.where(ahead >= 0, weights, 0.0)
            if k == 4:
                weights = jnp.where(ahead < 1024, weights, 0.0)
            add_in(g, weights, pair[:, 128:])

        if k == 0:
            one(0, 0)
            one(1, 1)
        else:

            @pl.when(z >= k)
            def _():
                one(0, 0)

            one(1, (z + 8 - k) // 8)

    exchange(0)
    og[z * 2 + c] = wo[...]
    o_start(0, 1, 2)
    for q in range(2):
        ag_a(q)
    exchange(1)
    w_own(0, 0)
    ag_a(2)
    ag_a(3)
    w_own(0, 1)
    for q in range(2):
        ag_b(q)
    w_step(0, 1)
    w_own(1, 0)
    w_own(1, 1)
    w_step(0, 2)
    o_step(0, 1)
    o_step(1, 1)
    w_step(1, 1)
    w_step(0, 3)
    ag_b(2)
    ag_b(3)
    w_step(1, 2)
    w_step(0, 4)
    o_step(1, 2)
    o_step(0, 2)
    for q in range(2):
        ag_done(q)
    w_done(0)
    project(0)
    keys = head_norm(acc[0:256, :128], k_gain[...]).astype(bf16)
    values = acc[0:256, 128:256].astype(bf16)
    for g in range(2):
        kvg[g, z, c, :, :128] = keys[g * 128 : (g + 1) * 128]
        kvg[g, z, c, :, 128:] = values[g * 128 : (g + 1) * 128]
    kv_start()
    w_step(1, 3)
    o_step(1, 3)
    kv_step(1)
    w_step(1, 4)
    o_step(0, 3)
    kv_step(2)
    w_done(1)
    project(1)
    for h in range(2):
        raw = acc[0:256, 256 + 128 * h : 384 + 128 * h]
        normed = (head_norm(raw, q_gain[...]) * QUERY_SCALE).astype(bf16)
        for g in range(2):
            qp[g, h * 128 : (h + 1) * 128, :] = normed[g * 128 : (g + 1) * 128]
    kv_step(3)
    o_step(1, 4)
    num[...] = jnp.zeros_like(num)
    tot[...] = jnp.zeros_like(tot)
    kv_done(0)
    prompt_step(0)
    kv_done(1)
    prompt_step(1)
    for q in (2, 3):
        ag_done(q)
    project_answers()
    keys = head_norm(acc[256:384, :128], k_gain[...]).astype(bf16)
    akv[:, :128] = keys
    akv[:, 128:] = acc[256:384, 128:256].astype(bf16)
    for h in range(2):
        raw = acc[256:384, 256 + 128 * h : 384 + 128 * h]
        normed = (head_norm(raw, q_gain[...]) * QUERY_SCALE).astype(bf16)
        for e in range(2):
            low = e * 128 + h * 64
            qa[low : low + 64, :] = normed[e * 64 : e * 64 + 64]
    kv_done(2)
    prompt_step(2)
    kv_step(4)
    row_ = lax.broadcasted_iota(jnp.int32, (256, 128), 0)
    col_ = lax.broadcasted_iota(jnp.int32, (256, 128), 1)
    own = scored(qa[...], akv[:, :128])
    own_seen = (row_ // 128 == col_ // 64) & (col_ % 64 <= row_ % 64)
    add_in(2, jnp.where(own_seen, own, 0.0), akv[:, 128:])
    kv_done(3)
    prompt_step(3)
    kv_done(4)
    prompt_step(4)
    for zz in range(4, 8):
        pair = kvg[1, zz].reshape(256, 256)
        weights = scored(qa[...], pair[:, :128])
        if zz == 4:
            weights = jnp.where(col > row % 64, weights, 0.0)
        add_in(2, weights, pair[:, 128:])


    for g in range(2):
        out = num[g] / jnp.sum(tot[g], axis=-1, keepdims=True)
        for h in range(2):
            att[g * 128 : (g + 1) * 128, h * 128 : (h + 1) * 128] = out[
                h * 128 : (h + 1) * 128
            ].astype(bf16)
    out = num[2] / jnp.sum(tot[2], axis=-1, keepdims=True)
    for e in range(2):
        for h in range(2):
            low = e * 128 + h * 64
            att[256 + e * 64 : 320 + e * 64, h * 128 : (h + 1) * 128] = out[
                low : low + 64
            ].astype(bf16)

    def rs_axes(q):
        if RS[q][2] == "x":
            return "x", "y", x, y
        return "y", "x", y, x

    def rs_a(q):
        start, width, axis = RS[q]
        cols_ = slice(start, start + width)
        left = jnp.dot(
            att[...],
            og[:, :, start : start + width].reshape(256, width),
            preferred_element_type=f32,
        )
        right = jnp.dot(
            att[...],
            og[:, :, HALF + start : HALF + start + width].reshape(256, width),
            preferred_element_type=f32,
        )
        for y_ in range(4):
            for x_ in range(4):
                i, k = (x_, y_) if axis == "x" else (y_, x_)
                p = y_ * 4 + x_
                sb[i, k, 0:16, cols_] = left[p * 16 : p * 16 + 16].astype(bf16)
                sb[i, k, 16:32, cols_] = right[p * 16 : p * 16 + 16].astype(bf16)
                low_ = 256 + p * 8
                sb[i, k, 32:48, cols_] = jnp.concatenate(
                    [left[low_ : low_ + 8], right[low_ : low_ + 8]], 0
                ).astype(bf16)
        first, _, mi, _ = rs_axes(q)
        cols_ = pl.ds(start, width)
        for w, d in enumerate((1, 3)):
            send(
                sb.at[(mi + 2) % 4, pl.ds(2 * w, 2), :, cols_],
                ra.at[w, :, :, cols_],
                rs_ss.at[q, w],
                rs_rs.at[q, w],
                peer(first, d),
            )

    def rs_b(q):
        start, width, _ = RS[q]
        first, _, mi, _ = rs_axes(q)
        cols_ = slice(start, start + width)
        for w, d in enumerate((1, 3)):
            arrived(ra.at[w, :, :, pl.ds(start, width)], rs_rs.at[q, w])
            i = (mi + d) % 4
            sb[i, 2 * w : 2 * w + 2, :, cols_] = (
                sb[i, 2 * w : 2 * w + 2, :, cols_].astype(f32)
                + ra[w, :, :, cols_].astype(f32)
            ).astype(bf16)
            send(
                sb.at[i, :, :, pl.ds(start, width)],
                r1.at[w, :, :, pl.ds(start, width)],
                rs_ss.at[q, 2 + w],
                rs_rs.at[q, 2 + w],
                peer(first, d),
            )

    def rs_c(q):
        start, width, _ = RS[q]
        _, second, mi, mj = rs_axes(q)
        cols_ = slice(start, start + width)
        for w in range(2):
            arrived(r1.at[w, :, :, pl.ds(start, width)], rs_rs.at[q, 2 + w])
        s2[:, :, cols_] = (
            sb[mi, :, :, cols_].astype(f32)
            + r1[0, :, :, cols_].astype(f32)
            + r1[1, :, :, cols_].astype(f32)
        ).astype(bf16)
        for d in ORDER:
            send(
                s2.at[(mj + d) % 4, :, pl.ds(start, width)],
                r2.at[d - 1, :, pl.ds(start, width)],
                rs_ss.at[q, 3 + d],
                rs_rs.at[q, 3 + d],
                peer(second, d),
            )

    def rs_d(q):
        start, width, _ = RS[q]
        _, _, _, mj = rs_axes(q)
        cols_ = slice(start, start + width)
        for d in ORDER:
            arrived(r2.at[d - 1, :, pl.ds(start, width)], rs_rs.at[q, 3 + d])
        total = s2[mj, :, cols_].astype(f32)
        for d in range(3):
            total = total + r2[d, :, cols_].astype(f32)
        mix[:, cols_] = total

    o_done()
    for q in range(len(RS)):
        rs_a(q)
    drain()
    for q in range(len(RS)):
        rs_b(q)
    for q in range(len(RS)):
        rs_c(q)
    for q in range(len(RS)):
        rs_d(q)

    gain = post_gain[...].reshape(1, D)

    def square_sum(part):
        return jnp.sum(part * part, axis=-1, keepdims=True)

    left, right = mix[0:16, :], mix[16:32, :]
    scale = lax.rsqrt((square_sum(left) + square_sum(right)) / D + EPS)
    p_out[:, :HALF] = (
        prompt[:, :HALF].astype(f32) + left * scale * gain[:, :HALF]
    ).astype(bf16)
    p_out[:, HALF:] = (
        prompt[:, HALF:].astype(f32) + right * scale * gain[:, HALF:]
    ).astype(bf16)
    left, right = mix[32:40, :], mix[40:48, :]
    scale = lax.rsqrt((square_sum(left) + square_sum(right)) / D + EPS)
    position = tp * 8 + lax.broadcasted_iota(jnp.int32, (8, HALF), 0)
    live = position < lens[0]
    a_out[:, :HALF] = jnp.where(
        live, answers[:, :HALF].astype(f32) + left * scale * gain[:, :HALF], 0.0
    ).astype(bf16)
    a_out[:, HALF:] = jnp.where(
        live, answers[:, HALF:].astype(f32) + right * scale * gain[:, HALF:], 0.0
    ).astype(bf16)

    drain()


def on_device(
    prompt,
    answers,
    answer_lengths,
    input_gain,
    query_weight,
    key_weight,
    value_weight,
    query_gain,
    key_gain,
    out_weight,
    post_gain,
):
    vmem = pl.BlockSpec(memory_space=pltpu.VMEM)
    dma = pltpu.SemaphoreType.DMA
    n_ag, n_rs = len(AG), len(RS)
    prompt_out, answer_out = pl.pallas_call(
        kernel,
        out_shape=(
            jax.ShapeDtypeStruct((16, D), bf16),
            jax.ShapeDtypeStruct((8, D), bf16),
        ),
        in_specs=[vmem, vmem, pl.BlockSpec(memory_space=pltpu.SMEM)] + [vmem] * 8,
        out_specs=(vmem, vmem),
        scratch_shapes=[
            pltpu.VMEM((2, 2, 2, PAD_W, 128), bf16),
            pltpu.VMEM((2, 3, PAD_W, 128), bf16),
            pltpu.VMEM((4, D, 128), bf16),
            pltpu.VMEM((4, 4, 48, HALF), bf16),
            pltpu.VMEM((384, 512), f32),
            pltpu.VMEM((2, 8, 2, 128, 256), bf16),
            pltpu.VMEM((128, 256), bf16),
            pltpu.VMEM((2, 256, 128), bf16),
            pltpu.VMEM((256, 128), bf16),
            pltpu.VMEM((3, 256, 128), f32),
            pltpu.VMEM((3, 256, 128), f32),
            pltpu.VMEM((384, 256), bf16),
            pltpu.VMEM((16, 16, D), bf16),
            pltpu.VMEM((4, 4, 48, HALF), bf16),
            pltpu.VMEM((2, 2, 48, HALF), bf16),
            pltpu.VMEM((2, 4, 48, HALF), bf16),
            pltpu.VMEM((4, 48, HALF), bf16),
            pltpu.VMEM((3, 48, HALF), bf16),
            pltpu.VMEM((48, HALF), f32),
            dma((2, 3)),
            dma((2, 3)),
            dma((2, 3, 16)),
            dma((2, 2, 16)),
            dma((3, 16)),
            dma((16,)),
            dma((3, 2, 8)),
            dma((2, 8, 2)),
            dma((n_ag, 7)),
            dma((n_ag, 7)),
            dma((n_rs, 7)),
            dma((n_rs, 7)),
        ],
        compiler_params=pltpu.CompilerParams(
            collective_id=0, has_side_effects=True, vmem_limit_bytes=56 * 1024 * 1024
        ),
        name="sublayer",
    )(
        prompt,
        answers[0],
        answer_lengths,
        input_gain,
        query_weight,
        key_weight,
        value_weight,
        query_gain[None],
        key_gain[None],
        out_weight,
        post_gain,
    )
    return prompt_out, answer_out[None]


def solution(mesh):
    placed = (
        P(("seq", "tp"), None),
        P("seq", "tp", None),
        P("seq"),
        P(),
        P("seq", "tp"),
        P("seq", "tp"),
        P("seq", "tp"),
        P(),
        P(),
        P(("tp", "seq"), None),
        P(),
    )
    return jax.shard_map(
        on_device,
        mesh=mesh,
        in_specs=placed,
        out_specs=(P(("seq", "tp"), None), P("seq", "tp", None)),
        check_vma=False,
    )
```

```python
import jax
import jax.numpy as jnp
from jax import lax
from jax.experimental import pallas as pl
from jax.experimental.pallas import tpu as pltpu
from jax.sharding import PartitionSpec as P

D = 5376
HALF = D // 2
HEAD = 128
ROWS_W = 168
PAIR_W = 2 * ROWS_W
PAD_W = 176
EPS = 1e-06
QUERY_SCALE = 168.0 ** (-0.5)
KC = 896

bf16 = jnp.bfloat16
f32 = jnp.float32

AG = (
    (0, 32, 0, 1280, "x"),
    (0, 32, 1280, 1408, "y"),
    (32, 16, 0, 1280, "x"),
    (32, 16, 1280, 1408, "y"),
)
RS = ((0, 640, "x"), (640, 640, "y"), (1280, 640, "x"), (1920, 768, "y"))
ORDER = (1, 3, 2)
O_REACH = (3, 4)


def kernel(
    prompt,
    answers,
    lens,
    in_gain,
    wq,
    wk,
    wv,
    q_gain,
    k_gain,
    wo,
    post_gain,
    p_out,
    a_out,
    st,
    rx,
    wg,
    xg,
    acc,
    kvg,
    akv,
    qp,
    qa,
    num,
    tot,
    att,
    og,
    sb,
    ra,
    r1,
    s2,
    r2,
    mix,
    e_ss,
    e_rs,
    w_ss,
    w_rs,
    o_ss,
    o_rs,
    kv_ss,
    kv_rs,
    ag_ss,
    ag_rs,
    rs_ss,
    rs_rs,
):
    seq = lax.axis_index("seq")
    tp = lax.axis_index("tp")
    yh, z, c = seq // 16, (seq // 2) % 8, seq % 2
    yl, x = tp // 4, tp % 4
    y = yh * 2 + yl

    def dev(y_, x_, z_, c_):
        return ((y_ // 2) * 16 + z_ * 2 + c_, (y_ % 2) * 4 + x_)

    sib = dev(y, x, z, 1 - c)
    z_to = (dev(y, x, (z + 1) % 8, c), dev(y, x, (z + 7) % 8, c))
    diag = dev((y + 2) % 4, x, z, 1 - c)

    def peer(axis, d):
        if axis == "x":
            return dev(y, (x + d) % 4, z, c)
        return dev((y + d) % 4, x, z, c)

    partners = [sib, *z_to, diag] + [peer(a, d) for a in "xy" for d in ORDER]
    barrier = pltpu.get_barrier_semaphore()
    for target in partners:
        pl.semaphore_signal(
            barrier, inc=1, device_id=target, device_id_type=pl.DeviceIdType.MESH
        )

    started = []

    def send(src, dst, send_sem, recv_sem, target):
        copy = pltpu.make_async_remote_copy(
            src_ref=src,
            dst_ref=dst,
            send_sem=send_sem,
            recv_sem=recv_sem,
            device_id=target,
            device_id_type=pl.DeviceIdType.MESH,
        )
        copy.start()
        started.append(copy)

    def arrived(dst, recv_sem):
        pltpu.make_async_remote_copy(
            src_ref=dst,
            dst_ref=dst,
            send_sem=e_ss.at[0, 0],
            recv_sem=recv_sem,
            device_id=sib,
            device_id_type=pl.DeviceIdType.MESH,
        ).wait_recv()

    for h in range(2):
        st[h, 0, 0, :ROWS_W, :] = wk[:, 128 * h : 128 * h + 128]
        st[h, 0, 1, :ROWS_W, :] = wv[:, 128 * h : 128 * h + 128]
        for i in range(2):
            low = 256 * h + 128 * i
            st[h, 1, i, :ROWS_W, :] = wq[:, low : low + 128]
    gain = in_gain[...].reshape(1, D)
    rows = prompt[...].astype(f32)
    rows = rows * lax.rsqrt(jnp.mean(rows * rows, axis=-1, keepdims=True) + EPS) * gain
    xg[y, x, 0:16, :] = rows[:, :HALF].astype(bf16)
    xg[y, x, 16:32, :] = rows[:, HALF:].astype(bf16)
    rows = answers[...].astype(f32)
    rows = rows * lax.rsqrt(jnp.mean(rows * rows, axis=-1, keepdims=True) + EPS) * gain
    xg[y, x, 32:48, :] = jnp.concatenate([rows[:, :HALF], rows[:, HALF:]], 0).astype(bf16)
    pl.semaphore_wait(barrier, len(partners))
    def exchange(f):
        send(st.at[yh, f, 1 - c], rx.at[f, 0], e_ss.at[f, 0], e_rs.at[f, 0], sib)
        send(
            st.at[1 - yh, f, c], rx.at[f, 1], e_ss.at[f, 1], e_rs.at[f, 1], peer("y", 2)
        )
        send(st.at[1 - yh, f, 1 - c], rx.at[f, 2], e_ss.at[f, 2], e_rs.at[f, 2], diag)

    def ag_one(q, y_, x_):
        row, count, start, width, _ = AG[q]
        return xg.at[y_, x_, pl.ds(row, count), pl.ds(start, width)]

    def ag_line(q, k):
        row, count, start, width, axis = AG[q]
        rows_, cols_ = pl.ds(row, count), pl.ds(start, width)
        if axis == "x":
            return xg.at[k, :, rows_, cols_]
        return xg.at[:, k, rows_, cols_]

    def ag_axes(q):
        if AG[q][4] == "x":
            return "x", "y", x, y
        return "y", "x", y, x

    def ag_a(q):
        first, _, _, _ = ag_axes(q)
        mine = ag_one(q, y, x)
        for d in ORDER:
            send(mine, mine, ag_ss.at[q, d - 1], ag_rs.at[q, d - 1], peer(first, d))

    def ag_b(q):
        first, second, _, own = ag_axes(q)
        for d in ORDER:
            if first == "x":
                piece = ag_one(q, y, (x + 4 - d) % 4)
            else:
                piece = ag_one(q, (y + 4 - d) % 4, x)
            arrived(piece, ag_rs.at[q, d - 1])
        mine = ag_line(q, own)
        for d in ORDER:
            send(mine, mine, ag_ss.at[q, 2 + d], ag_rs.at[q, 2 + d], peer(second, d))

    def ag_done(q):
        _, _, _, own = ag_axes(q)
        for d in ORDER:
            arrived(ag_line(q, (own + 4 - d) % 4), ag_rs.at[q, 2 + d])

    def w_block(f, core, m):
        return wg.at[2 * f + core, pl.ds(pl.multiple_of(m * PAIR_W, 16), PAIR_W), :]

    def w_index(h, dz):
        return ((yh + h) % 2) * 8 + (z + dz) % 8

    def w_send(f, m, way):
        piece = w_block(f, c, m)
        target = sib if way == 2 else z_to[way]
        send(piece, piece, w_ss.at[f, way, m], w_rs.at[f, c, m], target)

    def w_own(f, h):
        if h == 0:
            arrived(rx.at[f, 0], e_rs.at[f, 0])
            mine = st[yh, f, c, :ROWS_W, :].astype(f32)
            other = rx[f, 0, :ROWS_W, :].astype(f32)
        else:
            arrived(rx.at[f, 1], e_rs.at[f, 1])
            arrived(rx.at[f, 2], e_rs.at[f, 2])
            mine = rx[f, 1, :ROWS_W, :].astype(f32)
            other = rx[f, 2, :ROWS_W, :].astype(f32)
        low = jnp.where(c == 0, mine, other)
        high = jnp.where(c == 0, other, mine)
        m = w_index(h, 0)
        wg[2 * f + c, pl.ds(pl.multiple_of(m * PAIR_W, 16), PAIR_W), :] = (
            jnp.concatenate([low, high], 0).astype(bf16)
        )
        for way in range(3):
            w_send(f, m, way)

    def w_step(f, k):
        for h in range(2):
            for way in range(2):
                reach = 4 if h == way else 3
                if k <= reach:
                    m = w_index(h, 8 - k if way == 0 else k)
                    arrived(w_block(f, c, m), w_rs.at[f, c, m])
                    if k < reach:
                        w_send(f, m, way)
                    w_send(f, m, 2)

    def w_done(f):
        for m in range(16):
            arrived(w_block(f, 1 - c, m), w_rs.at[f, 1 - c, m])

    def o_send(slot, way):
        piece = og.at[slot]
        target = sib if way == 2 else z_to[way]
        send(piece, piece, o_ss.at[way, slot], o_rs.at[slot], target)

    def o_start(*ways):
        for way in ways:
            o_send(z * 2 + c, way)

    def o_step(way, k):
        slot = ((z + (8 - k if way == 0 else k)) % 8) * 2 + c
        arrived(og.at[slot], o_rs.at[slot])
        if k < O_REACH[way]:
            o_send(slot, way)
        o_send(slot, 2)

    def o_done():
        for zz in range(8):
            slot = zz * 2 + 1 - c
            arrived(og.at[slot], o_rs.at[slot])

    def drain():
        while started:
            started.pop(0).wait_send()

    def kv_send(g, zs, way):
        piece = kvg.at[g, zs, c]
        target = sib if way == 2 else z_to[way]
        send(piece, piece, kv_ss.at[way, g, zs], kv_rs.at[g, zs, c], target)

    def kv_start():
        for g in range(2):
            kv_send(g, z, 0)
        kv_send(1, z, 1)
        for g in range(2):
            kv_send(g, z, 2)

    def kv_step(k):
        zs = (z + 8 - k) % 8
        zn = (z + k) % 8
        for g in range(2):
            if k < 4 or g == 0:
                arrived(kvg.at[g, zs, c], kv_rs.at[g, zs, c])
                if k < 4 - g:
                    kv_send(g, zs, 0)
                kv_send(g, zs, 2)
        arrived(kvg.at[1, zn, c], kv_rs.at[1, zn, c])
        if k < 4:
            kv_send(1, zn, 1)
        kv_send(1, zn, 2)

    def kv_done(k):
        zs = (z + 8 - k) % 8
        zn = (z + k) % 8
        for g in range(2):
            arrived(kvg.at[g, zs, 1 - c], kv_rs.at[g, zs, 1 - c])
        if 0 < k < 4:
            arrived(kvg.at[1, zn, 1 - c], kv_rs.at[1, zn, 1 - c])

    def project(f):
        acc[0:256, 256 * f : 256 * f + 256] = jnp.zeros((256, 256), f32)
        for h in range(2):

            def body(i, carry):
                cols_ = pl.ds(pl.multiple_of(i * KC, 128), KC)
                krows = pl.ds(pl.multiple_of(h * HALF + i * KC, 128), KC)
                acc[0:256, 256 * f : 256 * f + 256] += jnp.dot(
                    xg[:, :, 16 * h : 16 * h + 16, cols_].reshape(256, KC),
                    jnp.concatenate([wg[2 * f, krows, :], wg[2 * f + 1, krows, :]], 1),
                    preferred_element_type=f32,
                )
                return carry

            lax.fori_loop(0, HALF // KC, body, 0)

    def project_answers():
        acc[256:384, :] = jnp.zeros((128, 512), f32)
        for h in range(2):

            def body(i, carry):
                cols_ = pl.ds(pl.multiple_of(i * KC, 128), KC)
                krows = pl.ds(pl.multiple_of(h * HALF + i * KC, 128), KC)
                tail = xg[:, :, 32:48, cols_].astype(f32)
                tail = tail[:, :, 8 * h : 8 * h + 8, :].reshape(128, KC).astype(bf16)
                acc[256:384, :] += jnp.dot(
                    tail,
                    jnp.concatenate([wg[i_, krows, :] for i_ in range(4)], 1),
                    preferred_element_type=f32,
                )
                return carry

            lax.fori_loop(0, HALF // KC, body, 0)

    def head_norm(raw, gains):
        return raw * lax.rsqrt(jnp.mean(raw * raw, axis=-1, keepdims=True) + EPS) * gains

    def scored(queries, keys_):
        return jnp.exp(
            lax.dot_general(
                queries, keys_, (((1,), (1,)), ((), ())), preferred_element_type=f32
            )
        )

    def add_in(slot, weights, values_):
        part = weights[:, :128]
        if weights.shape[1] == 256:
            part = part + weights[:, 128:]
        tot[slot] += part
        num[slot] += jnp.dot(weights.astype(bf16), values_, preferred_element_type=f32)

    row = lax.broadcasted_iota(jnp.int32, (256, 256), 0)
    col = lax.broadcasted_iota(jnp.int32, (256, 256), 1)

    def prompt_step(k):
        zs = (z + 8 - k) % 8
        ahead = c * 128 + 256 * k + row % 128 - col

        def one(g, source):
            pair = kvg[source, zs].reshape(256, 256)
            weights = scored(qp[g], pair[:, :128])
            if k == 0:
                weights = jnp.where(ahead >= 0, weights, 0.0)
            if k == 4:
                weights = jnp.where(ahead < 1024, weights, 0.0)
            add_in(g, weights, pair[:, 128:])

        if k == 0:
            one(0, 0)
            one(1, 1)
        else:

            @pl.when(z >= k)
            def _():
                one(0, 0)

            one(1, (z + 8 - k) // 8)

    exchange(0)
    og[z * 2 + c] = wo[...]
    o_start(0, 1, 2)
    for q in range(2):
        ag_a(q)
    exchange(1)
    w_own(0, 0)
    ag_a(2)
    ag_a(3)
    w_own(0, 1)
    for q in range(2):
        ag_b(q)
    w_step(0, 1)
    w_own(1, 0)
    w_own(1, 1)
    w_step(0, 2)
    o_step(0, 1)
    o_step(1, 1)
    w_step(1, 1)
    w_step(0, 3)
    ag_b(2)
    ag_b(3)
    w_step(1, 2)
    w_step(0, 4)
    o_step(1, 2)
    o_step(0, 2)
    for q in range(2):
        ag_done(q)
    w_done(0)
    project(0)
    keys = head_norm(acc[0:256, :128], k_gain[...]).astype(bf16)
    values = acc[0:256, 128:256].astype(bf16)
    for g in range(2):
        kvg[g, z, c, :, :128] = keys[g * 128 : (g + 1) * 128]
        kvg[g, z, c, :, 128:] = values[g * 128 : (g + 1) * 128]
    kv_start()
    w_step(1, 3)
    o_step(1, 3)
    kv_step(1)
    w_step(1, 4)
    o_step(0, 3)
    kv_step(2)
    w_done(1)
    project(1)
    for h in range(2):
        raw = acc[0:256, 256 + 128 * h : 384 + 128 * h]
        normed = (head_norm(raw, q_gain[...]) * QUERY_SCALE).astype(bf16)
        for g in range(2):
            qp[g, h * 128 : (h + 1) * 128, :] = normed[g * 128 : (g + 1) * 128]
    kv_step(3)
    o_step(1, 4)
    num[...] = jnp.zeros_like(num)
    tot[...] = jnp.zeros_like(tot)
    kv_done(0)
    prompt_step(0)
    kv_done(1)
    prompt_step(1)
    for q in (2, 3):
        ag_done(q)
    project_answers()
    keys = head_norm(acc[256:384, :128], k_gain[...]).astype(bf16)
    akv[:, :128] = keys
    akv[:, 128:] = acc[256:384, 128:256].astype(bf16)
    for h in range(2):
        raw = acc[256:384, 256 + 128 * h : 384 + 128 * h]
        normed = (head_norm(raw, q_gain[...]) * QUERY_SCALE).astype(bf16)
        for e in range(2):
            low = e * 128 + h * 64
            qa[low : low + 64, :] = normed[e * 64 : e * 64 + 64]
    kv_done(2)
    prompt_step(2)
    row_ = lax.broadcasted_iota(jnp.int32, (256, 128), 0)
    col_ = lax.broadcasted_iota(jnp.int32, (256, 128), 1)
    own = scored(qa[...], akv[:, :128])
    own_seen = (row_ // 128 == col_ // 64) & (col_ % 64 <= row_ % 64)
    add_in(2, jnp.where(own_seen, own, 0.0), akv[:, 128:])
    kv_done(3)
    prompt_step(3)
    kv_step(4)
    kv_done(4)
    prompt_step(4)
    for zz in range(4, 8):
        pair = kvg[1, zz].reshape(256, 256)
        weights = scored(qa[...], pair[:, :128])
        if zz == 4:
            weights = jnp.where(col > row % 64, weights, 0.0)
        add_in(2, weights, pair[:, 128:])


    for g in range(2):
        out = num[g] / jnp.sum(tot[g], axis=-1, keepdims=True)
        for h in range(2):
            att[g * 128 : (g + 1) * 128, h * 128 : (h + 1) * 128] = out[
                h * 128 : (h + 1) * 128
            ].astype(bf16)
    out = num[2] / jnp.sum(tot[2], axis=-1, keepdims=True)
    for e in range(2):
        for h in range(2):
            low = e * 128 + h * 64
            att[256 + e * 64 : 320 + e * 64, h * 128 : (h + 1) * 128] = out[
                low : low + 64
            ].astype(bf16)

    def rs_axes(q):
        if RS[q][2] == "x":
            return "x", "y", x, y
        return "y", "x", y, x

    def rs_a(q):
        start, width, axis = RS[q]
        cols_ = slice(start, start + width)
        left = jnp.dot(
            att[...],
            og[:, :, start : start + width].reshape(256, width),
            preferred_element_type=f32,
        )
        right = jnp.dot(
            att[...],
            og[:, :, HALF + start : HALF + start + width].reshape(256, width),
            preferred_element_type=f32,
        )
        for y_ in range(4):
            for x_ in range(4):
                i, k = (x_, y_) if axis == "x" else (y_, x_)
                p = y_ * 4 + x_
                sb[i, k, 0:16, cols_] = left[p * 16 : p * 16 + 16].astype(bf16)
                sb[i, k, 16:32, cols_] = right[p * 16 : p * 16 + 16].astype(bf16)
                low_ = 256 + p * 8
                sb[i, k, 32:48, cols_] = jnp.concatenate(
                    [left[low_ : low_ + 8], right[low_ : low_ + 8]], 0
                ).astype(bf16)
        first, _, mi, _ = rs_axes(q)
        cols_ = pl.ds(start, width)
        for w, d in enumerate((1, 3)):
            send(
                sb.at[(mi + 2) % 4, pl.ds(2 * w, 2), :, cols_],
                ra.at[w, :, :, cols_],
                rs_ss.at[q, w],
                rs_rs.at[q, w],
                peer(first, d),
            )

    def rs_b(q):
        start, width, _ = RS[q]
        first, _, mi, _ = rs_axes(q)
        cols_ = slice(start, start + width)
        for w, d in enumerate((1, 3)):
            arrived(ra.at[w, :, :, pl.ds(start, width)], rs_rs.at[q, w])
            i = (mi + d) % 4
            sb[i, 2 * w : 2 * w + 2, :, cols_] = (
                sb[i, 2 * w : 2 * w + 2, :, cols_].astype(f32)
                + ra[w, :, :, cols_].astype(f32)
            ).astype(bf16)
            send(
                sb.at[i, :, :, pl.ds(start, width)],
                r1.at[w, :, :, pl.ds(start, width)],
                rs_ss.at[q, 2 + w],
                rs_rs.at[q, 2 + w],
                peer(first, d),
            )

    def rs_c(q):
        start, width, _ = RS[q]
        _, second, mi, mj = rs_axes(q)
        cols_ = slice(start, start + width)
        for w in range(2):
            arrived(r1.at[w, :, :, pl.ds(start, width)], rs_rs.at[q, 2 + w])
        s2[:, :, cols_] = (
            sb[mi, :, :, cols_].astype(f32)
            + r1[0, :, :, cols_].astype(f32)
            + r1[1, :, :, cols_].astype(f32)
        ).astype(bf16)
        for d in ORDER:
            send(
                s2.at[(mj + d) % 4, :, pl.ds(start, width)],
                r2.at[d - 1, :, pl.ds(start, width)],
                rs_ss.at[q, 3 + d],
                rs_rs.at[q, 3 + d],
                peer(second, d),
            )

    def rs_d(q):
        start, width, _ = RS[q]
        _, _, _, mj = rs_axes(q)
        cols_ = slice(start, start + width)
        for d in ORDER:
            arrived(r2.at[d - 1, :, pl.ds(start, width)], rs_rs.at[q, 3 + d])
        total = s2[mj, :, cols_].astype(f32)
        for d in range(3):
            total = total + r2[d, :, cols_].astype(f32)
        mix[:, cols_] = total

    o_done()
    for q in range(len(RS)):
        rs_a(q)
    drain()
    for q in range(len(RS)):
        rs_b(q)
    for q in range(len(RS)):
        rs_c(q)
    for q in range(len(RS)):
        rs_d(q)

    gain = post_gain[...].reshape(1, D)

    def square_sum(part):
        return jnp.sum(part * part, axis=-1, keepdims=True)

    left, right = mix[0:16, :], mix[16:32, :]
    scale = lax.rsqrt((square_sum(left) + square_sum(right)) / D + EPS)
    p_out[:, :HALF] = (
        prompt[:, :HALF].astype(f32) + left * scale * gain[:, :HALF]
    ).astype(bf16)
    p_out[:, HALF:] = (
        prompt[:, HALF:].astype(f32) + right * scale * gain[:, HALF:]
    ).astype(bf16)
    left, right = mix[32:40, :], mix[40:48, :]
    scale = lax.rsqrt((square_sum(left) + square_sum(right)) / D + EPS)
    position = tp * 8 + lax.broadcasted_iota(jnp.int32, (8, HALF), 0)
    live = position < lens[0]
    a_out[:, :HALF] = jnp.where(
        live, answers[:, :HALF].astype(f32) + left * scale * gain[:, :HALF], 0.0
    ).astype(bf16)
    a_out[:, HALF:] = jnp.where(
        live, answers[:, HALF:].astype(f32) + right * scale * gain[:, HALF:], 0.0
    ).astype(bf16)

    drain()


def on_device(
    prompt,
    answers,
    answer_lengths,
    input_gain,
    query_weight,
    key_weight,
    value_weight,
    query_gain,
    key_gain,
    out_weight,
    post_gain,
):
    vmem = pl.BlockSpec(memory_space=pltpu.VMEM)
    dma = pltpu.SemaphoreType.DMA
    n_ag, n_rs = len(AG), len(RS)
    prompt_out, answer_out = pl.pallas_call(
        kernel,
        out_shape=(
            jax.ShapeDtypeStruct((16, D), bf16),
            jax.ShapeDtypeStruct((8, D), bf16),
        ),
        in_specs=[vmem, vmem, pl.BlockSpec(memory_space=pltpu.SMEM)] + [vmem] * 8,
        out_specs=(vmem, vmem),
        scratch_shapes=[
            pltpu.VMEM((2, 2, 2, PAD_W, 128), bf16),
            pltpu.VMEM((2, 3, PAD_W, 128), bf16),
            pltpu.VMEM((4, D, 128), bf16),
            pltpu.VMEM((4, 4, 48, HALF), bf16),
            pltpu.VMEM((384, 512), f32),
            pltpu.VMEM((2, 8, 2, 128, 256), bf16),
            pltpu.VMEM((128, 256), bf16),
            pltpu.VMEM((2, 256, 128), bf16),
            pltpu.VMEM((256, 128), bf16),
            pltpu.VMEM((3, 256, 128), f32),
            pltpu.VMEM((3, 256, 128), f32),
            pltpu.VMEM((384, 256), bf16),
            pltpu.VMEM((16, 16, D), bf16),
            pltpu.VMEM((4, 4, 48, HALF), bf16),
            pltpu.VMEM((2, 2, 48, HALF), bf16),
            pltpu.VMEM((2, 4, 48, HALF), bf16),
            pltpu.VMEM((4, 48, HALF), bf16),
            pltpu.VMEM((3, 48, HALF), bf16),
            pltpu.VMEM((48, HALF), f32),
            dma((2, 3)),
            dma((2, 3)),
            dma((2, 3, 16)),
            dma((2, 2, 16)),
            dma((3, 16)),
            dma((16,)),
            dma((3, 2, 8)),
            dma((2, 8, 2)),
            dma((n_ag, 7)),
            dma((n_ag, 7)),
            dma((n_rs, 7)),
            dma((n_rs, 7)),
        ],
        compiler_params=pltpu.CompilerParams(
            collective_id=0, has_side_effects=True, vmem_limit_bytes=56 * 1024 * 1024
        ),
        name="sublayer",
    )(
        prompt,
        answers[0],
        answer_lengths,
        input_gain,
        query_weight,
        key_weight,
        value_weight,
        query_gain[None],
        key_gain[None],
        out_weight,
        post_gain,
    )
    return prompt_out, answer_out[None]


def solution(mesh):
    placed = (
        P(("seq", "tp"), None),
        P("seq", "tp", None),
        P("seq"),
        P(),
        P("seq", "tp"),
        P("seq", "tp"),
        P("seq", "tp"),
        P(),
        P(),
        P(("tp", "seq"), None),
        P(),
    )
    return jax.shard_map(
        on_device,
        mesh=mesh,
        in_specs=placed,
        out_specs=(P(("seq", "tp"), None), P("seq", "tp", None)),
        check_vma=False,
    )
```

```python
import jax
import jax.numpy as jnp
from jax import lax
from jax.experimental import pallas as pl
from jax.experimental.pallas import tpu as pltpu
from jax.sharding import PartitionSpec as P

D = 5376
HALF = D // 2
HEAD = 128
ROWS_W = 168
PAIR_W = 2 * ROWS_W
PAD_W = 176
EPS = 1e-06
QUERY_SCALE = 168.0 ** (-0.5)
KC = 896

bf16 = jnp.bfloat16
f32 = jnp.float32

AG = (
    (0, 32, 0, 1280, "x"),
    (0, 32, 1280, 1408, "y"),
    (32, 16, 0, 1280, "x"),
    (32, 16, 1280, 1408, "y"),
)
RS = ((0, 640, "x"), (640, 640, "y"), (1280, 640, "x"), (1920, 768, "y"))
ORDER = (1, 3, 2)
O_REACH = (3, 4)


def kernel(
    prompt,
    answers,
    lens,
    in_gain,
    wq,
    wk,
    wv,
    q_gain,
    k_gain,
    wo,
    post_gain,
    p_out,
    a_out,
    st,
    rx,
    wg,
    xg,
    acc,
    kvg,
    akv,
    qp,
    qa,
    num,
    tot,
    att,
    og,
    sb,
    ra,
    r1,
    s2,
    r2,
    mix,
    e_ss,
    e_rs,
    w_ss,
    w_rs,
    o_ss,
    o_rs,
    kv_ss,
    kv_rs,
    ag_ss,
    ag_rs,
    rs_ss,
    rs_rs,
):
    seq = lax.axis_index("seq")
    tp = lax.axis_index("tp")
    yh, z, c = seq // 16, (seq // 2) % 8, seq % 2
    yl, x = tp // 4, tp % 4
    y = yh * 2 + yl

    def dev(y_, x_, z_, c_):
        return ((y_ // 2) * 16 + z_ * 2 + c_, (y_ % 2) * 4 + x_)

    sib = dev(y, x, z, 1 - c)
    z_to = (dev(y, x, (z + 1) % 8, c), dev(y, x, (z + 7) % 8, c))
    diag = dev((y + 2) % 4, x, z, 1 - c)

    def peer(axis, d):
        if axis == "x":
            return dev(y, (x + d) % 4, z, c)
        return dev((y + d) % 4, x, z, c)

    partners = [sib, *z_to, diag] + [peer(a, d) for a in "xy" for d in ORDER]
    barrier = pltpu.get_barrier_semaphore()
    for target in partners:
        pl.semaphore_signal(
            barrier, inc=1, device_id=target, device_id_type=pl.DeviceIdType.MESH
        )

    started = []

    def send(src, dst, send_sem, recv_sem, target):
        copy = pltpu.make_async_remote_copy(
            src_ref=src,
            dst_ref=dst,
            send_sem=send_sem,
            recv_sem=recv_sem,
            device_id=target,
            device_id_type=pl.DeviceIdType.MESH,
        )
        copy.start()
        started.append(copy)

    def arrived(dst, recv_sem):
        pltpu.make_async_remote_copy(
            src_ref=dst,
            dst_ref=dst,
            send_sem=e_ss.at[0, 0],
            recv_sem=recv_sem,
            device_id=sib,
            device_id_type=pl.DeviceIdType.MESH,
        ).wait_recv()

    for h in range(2):
        st[h, 0, 0, :ROWS_W, :] = wk[:, 128 * h : 128 * h + 128]
        st[h, 0, 1, :ROWS_W, :] = wv[:, 128 * h : 128 * h + 128]
        for i in range(2):
            low = 256 * h + 128 * i
            st[h, 1, i, :ROWS_W, :] = wq[:, low : low + 128]
    gain = in_gain[...].reshape(1, D)
    rows = prompt[...].astype(f32)
    rows = rows * lax.rsqrt(jnp.mean(rows * rows, axis=-1, keepdims=True) + EPS) * gain
    xg[y, x, 0:16, :] = rows[:, :HALF].astype(bf16)
    xg[y, x, 16:32, :] = rows[:, HALF:].astype(bf16)
    rows = answers[...].astype(f32)
    rows = rows * lax.rsqrt(jnp.mean(rows * rows, axis=-1, keepdims=True) + EPS) * gain
    xg[y, x, 32:48, :] = jnp.concatenate([rows[:, :HALF], rows[:, HALF:]], 0).astype(bf16)
    pl.semaphore_wait(barrier, len(partners))
    def exchange(f):
        send(st.at[yh, f, 1 - c], rx.at[f, 0], e_ss.at[f, 0], e_rs.at[f, 0], sib)
        send(
            st.at[1 - yh, f, c], rx.at[f, 1], e_ss.at[f, 1], e_rs.at[f, 1], peer("y", 2)
        )
        send(st.at[1 - yh, f, 1 - c], rx.at[f, 2], e_ss.at[f, 2], e_rs.at[f, 2], diag)

    def ag_one(q, y_, x_):
        row, count, start, width, _ = AG[q]
        return xg.at[y_, x_, pl.ds(row, count), pl.ds(start, width)]

    def ag_line(q, k):
        row, count, start, width, axis = AG[q]
        rows_, cols_ = pl.ds(row, count), pl.ds(start, width)
        if axis == "x":
            return xg.at[k, :, rows_, cols_]
        return xg.at[:, k, rows_, cols_]

    def ag_axes(q):
        if AG[q][4] == "x":
            return "x", "y", x, y
        return "y", "x", y, x

    def ag_a(q):
        first, _, _, _ = ag_axes(q)
        mine = ag_one(q, y, x)
        for d in ORDER:
            send(mine, mine, ag_ss.at[q, d - 1], ag_rs.at[q, d - 1], peer(first, d))

    def ag_b(q):
        first, second, _, own = ag_axes(q)
        for d in ORDER:
            if first == "x":
                piece = ag_one(q, y, (x + 4 - d) % 4)
            else:
                piece = ag_one(q, (y + 4 - d) % 4, x)
            arrived(piece, ag_rs.at[q, d - 1])
        mine = ag_line(q, own)
        for d in ORDER:
            send(mine, mine, ag_ss.at[q, 2 + d], ag_rs.at[q, 2 + d], peer(second, d))

    def ag_done(q):
        _, _, _, own = ag_axes(q)
        for d in ORDER:
            arrived(ag_line(q, (own + 4 - d) % 4), ag_rs.at[q, 2 + d])

    def w_block(f, core, m):
        return wg.at[2 * f + core, pl.ds(pl.multiple_of(m * PAIR_W, 16), PAIR_W), :]

    def w_index(h, dz):
        return ((yh + h) % 2) * 8 + (z + dz) % 8

    def w_send(f, m, way):
        piece = w_block(f, c, m)
        target = sib if way == 2 else z_to[way]
        send(piece, piece, w_ss.at[f, way, m], w_rs.at[f, c, m], target)

    def w_own(f, h):
        if h == 0:
            arrived(rx.at[f, 0], e_rs.at[f, 0])
            mine = st[yh, f, c, :ROWS_W, :].astype(f32)
            other = rx[f, 0, :ROWS_W, :].astype(f32)
        else:
            arrived(rx.at[f, 1], e_rs.at[f, 1])
            arrived(rx.at[f, 2], e_rs.at[f, 2])
            mine = rx[f, 1, :ROWS_W, :].astype(f32)
            other = rx[f, 2, :ROWS_W, :].astype(f32)
        low = jnp.where(c == 0, mine, other)
        high = jnp.where(c == 0, other, mine)
        m = w_index(h, 0)
        wg[2 * f + c, pl.ds(pl.multiple_of(m * PAIR_W, 16), PAIR_W), :] = (
            jnp.concatenate([low, high], 0).astype(bf16)
        )
        for way in range(3):
            w_send(f, m, way)

    def w_step(f, k):
        for h in range(2):
            for way in range(2):
                reach = 4 if h == way else 3
                if k <= reach:
                    m = w_index(h, 8 - k if way == 0 else k)
                    arrived(w_block(f, c, m), w_rs.at[f, c, m])
                    if k < reach:
                        w_send(f, m, way)
                    w_send(f, m, 2)

    def w_done(f):
        for m in range(16):
            arrived(w_block(f, 1 - c, m), w_rs.at[f, 1 - c, m])

    def o_send(slot, way):
        piece = og.at[slot]
        target = sib if way == 2 else z_to[way]
        send(piece, piece, o_ss.at[way, slot], o_rs.at[slot], target)

    def o_start(*ways):
        for way in ways:
            o_send(z * 2 + c, way)

    def o_step(way, k):
        slot = ((z + (8 - k if way == 0 else k)) % 8) * 2 + c
        arrived(og.at[slot], o_rs.at[slot])
        if k < O_REACH[way]:
            o_send(slot, way)
        o_send(slot, 2)

    def o_done():
        for zz in range(8):
            slot = zz * 2 + 1 - c
            arrived(og.at[slot], o_rs.at[slot])

    def drain():
        while started:
            started.pop(0).wait_send()

    def kv_send(g, zs, way):
        piece = kvg.at[g, zs, c]
        target = sib if way == 2 else z_to[way]
        send(piece, piece, kv_ss.at[way, g, zs], kv_rs.at[g, zs, c], target)

    def kv_start():
        for g in range(2):
            kv_send(g, z, 0)
        kv_send(1, z, 1)
        for g in range(2):
            kv_send(g, z, 2)

    def kv_step(k):
        zs = (z + 8 - k) % 8
        zn = (z + k) % 8
        for g in range(2):
            if k < 4 or g == 0:
                arrived(kvg.at[g, zs, c], kv_rs.at[g, zs, c])
                if k < 4 - g:
                    kv_send(g, zs, 0)
                kv_send(g, zs, 2)
        arrived(kvg.at[1, zn, c], kv_rs.at[1, zn, c])
        if k < 4:
            kv_send(1, zn, 1)
        kv_send(1, zn, 2)

    def kv_done(k):
        zs = (z + 8 - k) % 8
        zn = (z + k) % 8
        for g in range(2):
            arrived(kvg.at[g, zs, 1 - c], kv_rs.at[g, zs, 1 - c])
        if 0 < k < 4:
            arrived(kvg.at[1, zn, 1 - c], kv_rs.at[1, zn, 1 - c])

    def project(f):
        acc[0:256, 256 * f : 256 * f + 256] = jnp.zeros((256, 256), f32)
        for h in range(2):

            def body(i, carry):
                cols_ = pl.ds(pl.multiple_of(i * KC, 128), KC)
                krows = pl.ds(pl.multiple_of(h * HALF + i * KC, 128), KC)
                acc[0:256, 256 * f : 256 * f + 256] += jnp.dot(
                    xg[:, :, 16 * h : 16 * h + 16, cols_].reshape(256, KC),
                    jnp.concatenate([wg[2 * f, krows, :], wg[2 * f + 1, krows, :]], 1),
                    preferred_element_type=f32,
                )
                return carry

            lax.fori_loop(0, HALF // KC, body, 0)

    def project_answers():
        acc[256:384, :] = jnp.zeros((128, 512), f32)
        for h in range(2):

            def body(i, carry):
                cols_ = pl.ds(pl.multiple_of(i * KC, 128), KC)
                krows = pl.ds(pl.multiple_of(h * HALF + i * KC, 128), KC)
                tail = xg[:, :, 32:48, cols_].astype(f32)
                tail = tail[:, :, 8 * h : 8 * h + 8, :].reshape(128, KC).astype(bf16)
                acc[256:384, :] += jnp.dot(
                    tail,
                    jnp.concatenate([wg[i_, krows, :] for i_ in range(4)], 1),
                    preferred_element_type=f32,
                )
                return carry

            lax.fori_loop(0, HALF // KC, body, 0)

    def head_norm(raw, gains):
        return raw * lax.rsqrt(jnp.mean(raw * raw, axis=-1, keepdims=True) + EPS) * gains

    def scored(queries, keys_):
        return jnp.exp(
            lax.dot_general(
                queries, keys_, (((1,), (1,)), ((), ())), preferred_element_type=f32
            )
        )

    def add_in(slot, weights, values_):
        part = weights[:, :128]
        if weights.shape[1] == 256:
            part = part + weights[:, 128:]
        tot[slot] += part
        num[slot] += jnp.dot(weights.astype(bf16), values_, preferred_element_type=f32)

    row = lax.broadcasted_iota(jnp.int32, (256, 256), 0)
    col = lax.broadcasted_iota(jnp.int32, (256, 256), 1)

    def prompt_step(k):
        zs = (z + 8 - k) % 8
        ahead = c * 128 + 256 * k + row % 128 - col

        def one(g, source):
            pair = kvg[source, zs].reshape(256, 256)
            weights = scored(qp[g], pair[:, :128])
            if k == 0:
                weights = jnp.where(ahead >= 0, weights, 0.0)
            if k == 4:
                weights = jnp.where(ahead < 1024, weights, 0.0)
            add_in(g, weights, pair[:, 128:])

        if k == 0:
            one(0, 0)
            one(1, 1)
        else:

            @pl.when(z >= k)
            def _():
                one(0, 0)

            one(1, (z + 8 - k) // 8)

    def window_step(dz):
        zz = (z + dz) % 8

        @pl.when(zz >= 4)
        def _():
            pair = kvg[1, zz].reshape(256, 256)
            weights = scored(qa[...], pair[:, :128])
            seen = col + 64 * (zz - 4) > row % 64
            add_in(2, jnp.where(seen, weights, 0.0), pair[:, 128:])

    exchange(0)
    og[z * 2 + c] = wo[...]
    o_start(0, 1, 2)
    for q in range(2):
        ag_a(q)
    exchange(1)
    w_own(0, 0)
    ag_a(2)
    ag_a(3)
    w_own(0, 1)
    for q in range(2):
        ag_b(q)
    w_step(0, 1)
    w_own(1, 0)
    w_own(1, 1)
    w_step(0, 2)
    o_step(0, 1)
    o_step(1, 1)
    w_step(1, 1)
    w_step(0, 3)
    ag_b(2)
    ag_b(3)
    w_step(1, 2)
    w_step(0, 4)
    o_step(1, 2)
    o_step(0, 2)
    for q in range(2):
        ag_done(q)
    w_done(0)
    project(0)
    keys = head_norm(acc[0:256, :128], k_gain[...]).astype(bf16)
    values = acc[0:256, 128:256].astype(bf16)
    for g in range(2):
        kvg[g, z, c, :, :128] = keys[g * 128 : (g + 1) * 128]
        kvg[g, z, c, :, 128:] = values[g * 128 : (g + 1) * 128]
    kv_start()
    w_step(1, 3)
    o_step(1, 3)
    kv_step(1)
    w_step(1, 4)
    o_step(0, 3)
    kv_step(2)
    w_done(1)
    project(1)
    for h in range(2):
        raw = acc[0:256, 256 + 128 * h : 384 + 128 * h]
        normed = (head_norm(raw, q_gain[...]) * QUERY_SCALE).astype(bf16)
        for g in range(2):
            qp[g, h * 128 : (h + 1) * 128, :] = normed[g * 128 : (g + 1) * 128]
    kv_step(3)
    o_step(1, 4)
    num[...] = jnp.zeros_like(num)
    tot[...] = jnp.zeros_like(tot)
    kv_done(0)
    prompt_step(0)
    kv_done(1)
    prompt_step(1)
    for q in (2, 3):
        ag_done(q)
    project_answers()
    keys = head_norm(acc[256:384, :128], k_gain[...]).astype(bf16)
    akv[:, :128] = keys
    akv[:, 128:] = acc[256:384, 128:256].astype(bf16)
    for h in range(2):
        raw = acc[256:384, 256 + 128 * h : 384 + 128 * h]
        normed = (head_norm(raw, q_gain[...]) * QUERY_SCALE).astype(bf16)
        for e in range(2):
            low = e * 128 + h * 64
            qa[low : low + 64, :] = normed[e * 64 : e * 64 + 64]
    kv_done(2)
    prompt_step(2)
    row_ = lax.broadcasted_iota(jnp.int32, (256, 128), 0)
    col_ = lax.broadcasted_iota(jnp.int32, (256, 128), 1)
    own = scored(qa[...], akv[:, :128])
    own_seen = (row_ // 128 == col_ // 64) & (col_ % 64 <= row_ % 64)
    add_in(2, jnp.where(own_seen, own, 0.0), akv[:, 128:])
    kv_done(3)
    prompt_step(3)
    for dz in (0, 1, 2, 3, 5, 6, 7):
        window_step(dz)
    kv_step(4)
    kv_done(4)
    prompt_step(4)
    window_step(4)


    for g in range(2):
        out = num[g] / jnp.sum(tot[g], axis=-1, keepdims=True)
        for h in range(2):
            att[g * 128 : (g + 1) * 128, h * 128 : (h + 1) * 128] = out[
                h * 128 : (h + 1) * 128
            ].astype(bf16)
    out = num[2] / jnp.sum(tot[2], axis=-1, keepdims=True)
    for e in range(2):
        for h in range(2):
            low = e * 128 + h * 64
            att[256 + e * 64 : 320 + e * 64, h * 128 : (h + 1) * 128] = out[
                low : low + 64
            ].astype(bf16)

    def rs_axes(q):
        if RS[q][2] == "x":
            return "x", "y", x, y
        return "y", "x", y, x

    def rs_a(q):
        start, width, axis = RS[q]
        cols_ = slice(start, start + width)
        left = jnp.dot(
            att[...],
            og[:, :, start : start + width].reshape(256, width),
            preferred_element_type=f32,
        )
        right = jnp.dot(
            att[...],
            og[:, :, HALF + start : HALF + start + width].reshape(256, width),
            preferred_element_type=f32,
        )
        for y_ in range(4):
            for x_ in range(4):
                i, k = (x_, y_) if axis == "x" else (y_, x_)
                p = y_ * 4 + x_
                sb[i, k, 0:16, cols_] = left[p * 16 : p * 16 + 16].astype(bf16)
                sb[i, k, 16:32, cols_] = right[p * 16 : p * 16 + 16].astype(bf16)
                low_ = 256 + p * 8
                sb[i, k, 32:48, cols_] = jnp.concatenate(
                    [left[low_ : low_ + 8], right[low_ : low_ + 8]], 0
                ).astype(bf16)
        first, _, mi, _ = rs_axes(q)
        cols_ = pl.ds(start, width)
        for w, d in enumerate((1, 3)):
            send(
                sb.at[(mi + 2) % 4, pl.ds(2 * w, 2), :, cols_],
                ra.at[w, :, :, cols_],
                rs_ss.at[q, w],
                rs_rs.at[q, w],
                peer(first, d),
            )

    def rs_b(q):
        start, width, _ = RS[q]
        first, _, mi, _ = rs_axes(q)
        cols_ = slice(start, start + width)
        for w, d in enumerate((1, 3)):
            arrived(ra.at[w, :, :, pl.ds(start, width)], rs_rs.at[q, w])
            i = (mi + d) % 4
            sb[i, 2 * w : 2 * w + 2, :, cols_] = (
                sb[i, 2 * w : 2 * w + 2, :, cols_].astype(f32)
                + ra[w, :, :, cols_].astype(f32)
            ).astype(bf16)
            send(
                sb.at[i, :, :, pl.ds(start, width)],
                r1.at[w, :, :, pl.ds(start, width)],
                rs_ss.at[q, 2 + w],
                rs_rs.at[q, 2 + w],
                peer(first, d),
            )

    def rs_c(q):
        start, width, _ = RS[q]
        _, second, mi, mj = rs_axes(q)
        cols_ = slice(start, start + width)
        for w in range(2):
            arrived(r1.at[w, :, :, pl.ds(start, width)], rs_rs.at[q, 2 + w])
        s2[:, :, cols_] = (
            sb[mi, :, :, cols_].astype(f32)
            + r1[0, :, :, cols_].astype(f32)
            + r1[1, :, :, cols_].astype(f32)
        ).astype(bf16)
        for d in ORDER:
            send(
                s2.at[(mj + d) % 4, :, pl.ds(start, width)],
                r2.at[d - 1, :, pl.ds(start, width)],
                rs_ss.at[q, 3 + d],
                rs_rs.at[q, 3 + d],
                peer(second, d),
            )

    def rs_d(q):
        start, width, _ = RS[q]
        _, _, _, mj = rs_axes(q)
        cols_ = slice(start, start + width)
        for d in ORDER:
            arrived(r2.at[d - 1, :, pl.ds(start, width)], rs_rs.at[q, 3 + d])
        total = s2[mj, :, cols_].astype(f32)
        for d in range(3):
            total = total + r2[d, :, cols_].astype(f32)
        mix[:, cols_] = total

    o_done()
    for q in range(len(RS)):
        rs_a(q)
    drain()
    for q in range(len(RS)):
        rs_b(q)
    for q in range(len(RS)):
        rs_c(q)
    for q in range(len(RS)):
        rs_d(q)

    gain = post_gain[...].reshape(1, D)

    def square_sum(part):
        return jnp.sum(part * part, axis=-1, keepdims=True)

    left, right = mix[0:16, :], mix[16:32, :]
    scale = lax.rsqrt((square_sum(left) + square_sum(right)) / D + EPS)
    p_out[:, :HALF] = (
        prompt[:, :HALF].astype(f32) + left * scale * gain[:, :HALF]
    ).astype(bf16)
    p_out[:, HALF:] = (
        prompt[:, HALF:].astype(f32) + right * scale * gain[:, HALF:]
    ).astype(bf16)
    left, right = mix[32:40, :], mix[40:48, :]
    scale = lax.rsqrt((square_sum(left) + square_sum(right)) / D + EPS)
    position = tp * 8 + lax.broadcasted_iota(jnp.int32, (8, HALF), 0)
    live = position < lens[0]
    a_out[:, :HALF] = jnp.where(
        live, answers[:, :HALF].astype(f32) + left * scale * gain[:, :HALF], 0.0
    ).astype(bf16)
    a_out[:, HALF:] = jnp.where(
        live, answers[:, HALF:].astype(f32) + right * scale * gain[:, HALF:], 0.0
    ).astype(bf16)

    drain()


def on_device(
    prompt,
    answers,
    answer_lengths,
    input_gain,
    query_weight,
    key_weight,
    value_weight,
    query_gain,
    key_gain,
    out_weight,
    post_gain,
):
    vmem = pl.BlockSpec(memory_space=pltpu.VMEM)
    dma = pltpu.SemaphoreType.DMA
    n_ag, n_rs = len(AG), len(RS)
    prompt_out, answer_out = pl.pallas_call(
        kernel,
        out_shape=(
            jax.ShapeDtypeStruct((16, D), bf16),
            jax.ShapeDtypeStruct((8, D), bf16),
        ),
        in_specs=[vmem, vmem, pl.BlockSpec(memory_space=pltpu.SMEM)] + [vmem] * 8,
        out_specs=(vmem, vmem),
        scratch_shapes=[
            pltpu.VMEM((2, 2, 2, PAD_W, 128), bf16),
            pltpu.VMEM((2, 3, PAD_W, 128), bf16),
            pltpu.VMEM((4, D, 128), bf16),
            pltpu.VMEM((4, 4, 48, HALF), bf16),
            pltpu.VMEM((384, 512), f32),
            pltpu.VMEM((2, 8, 2, 128, 256), bf16),
            pltpu.VMEM((128, 256), bf16),
            pltpu.VMEM((2, 256, 128), bf16),
            pltpu.VMEM((256, 128), bf16),
            pltpu.VMEM((3, 256, 128), f32),
            pltpu.VMEM((3, 256, 128), f32),
            pltpu.VMEM((384, 256), bf16),
            pltpu.VMEM((16, 16, D), bf16),
            pltpu.VMEM((4, 4, 48, HALF), bf16),
            pltpu.VMEM((2, 2, 48, HALF), bf16),
            pltpu.VMEM((2, 4, 48, HALF), bf16),
            pltpu.VMEM((4, 48, HALF), bf16),
            pltpu.VMEM((3, 48, HALF), bf16),
            pltpu.VMEM((48, HALF), f32),
            dma((2, 3)),
            dma((2, 3)),
            dma((2, 3, 16)),
            dma((2, 2, 16)),
            dma((3, 16)),
            dma((16,)),
            dma((3, 2, 8)),
            dma((2, 8, 2)),
            dma((n_ag, 7)),
            dma((n_ag, 7)),
            dma((n_rs, 7)),
            dma((n_rs, 7)),
        ],
        compiler_params=pltpu.CompilerParams(
            collective_id=0, has_side_effects=True, vmem_limit_bytes=56 * 1024 * 1024
        ),
        name="sublayer",
    )(
        prompt,
        answers[0],
        answer_lengths,
        input_gain,
        query_weight,
        key_weight,
        value_weight,
        query_gain[None],
        key_gain[None],
        out_weight,
        post_gain,
    )
    return prompt_out, answer_out[None]


def solution(mesh):
    placed = (
        P(("seq", "tp"), None),
        P("seq", "tp", None),
        P("seq"),
        P(),
        P("seq", "tp"),
        P("seq", "tp"),
        P("seq", "tp"),
        P(),
        P(),
        P(("tp", "seq"), None),
        P(),
    )
    return jax.shard_map(
        on_device,
        mesh=mesh,
        in_specs=placed,
        out_specs=(P(("seq", "tp"), None), P("seq", "tp", None)),
        check_vma=False,
    )
```
